32 devices in a mesh: grp: 2 (over y), lat: 4 (over z), lon: 2 (over x), role: 2 (over core).
Axes of the slice: x: 2, y: 2, z: 4, core: 2. Of those that a mesh axis runs over, the one named last changes fastest.
Arguments:
- eastern_edge_current: float32 [8, 128, 256], P('lon', ('grp', 'lat', 'role')), parts along dimension 1, may hold values from -1.5 to 1.5
- northern_edge_current: float32 [8, 128, 256], P('lon', ('grp', 'lat', 'role')), parts along dimension 1, may hold values from -1.5 to 1.5
- thermal_anomaly: float32 [8, 128, 256], P('lon', ('grp', 'lat', 'role')), parts along dimension 1, may hold values from -6 to 6
- prior_warming: float32 [8, 128, 256], P('lon', ('grp', 'lat', 'role')), parts along dimension 1, may hold values from 0 to 0.5
- solute_fields: float32 [24, 8, 128, 256], P(None, None, ('grp', 'lat', 'role'), 'lon'), parts along dimension 2, may hold values from -6 to 6
- submerged_layer_count: int32 [128, 256], P(('grp', 'lat', 'role')), parts along dimension 0, may hold values from 0 to 8
- reaction_rates: float32 [24, 24], replicated, may hold values from -1.25 to 1.25
Outputs:
- u_out: float32 [8, 128, 256], P('lon', ('grp', 'lat', 'role')), parts along dimension 1
- v_out: float32 [8, 128, 256], P('lon', ('grp', 'lat', 'role')), parts along dimension 1
- temp_out: float32 [8, 128, 256], P('lon', ('grp', 'lat', 'role')), parts along dimension 1
- heating_out: float32 [8, 128, 256], P('lon', ('grp', 'lat', 'role')), parts along dimension 1
- tracers_out: float32 [24, 8, 128, 256], P(None, None, ('grp', 'lat', 'role'), 'lon'), parts along dimension 2
The draws below stay inside these ranges and needn't reach their ends.
There are 2 independent parts, one for each index of `grp`. The reference program is written for one: setup_inputs(seed, part) draws one part's arguments, and reference() takes and returns one part's arrays. A program takes and returns all parts, laid end to end along the dimension named above; an argument that names none is the same for every part. Nothing has to cross between parts.
All inputs are finite; a program needn't handle non-finite values.
Results may differ from the reference program's by a relative error of at most 0.0001.
Values sent between devices are 32-bit elements; how exact they have to be, the bound alone decides.
A program may use at most 64 MiB of HBM per device.

```python
import jax
import jax.numpy as jnp
from jax import lax

TR = 24
DEPTH_LAYERS = 8
STEPS = 2
GRID_PARALLELS = 64
GRID_MERIDIANS = 256


def place_ends(array, key, low, high):
    longest = array.shape.index(max(array.shape))
    spots = []
    for shift in (0, 1):
        where = [jax.random.randint(jax.random.fold_in(key, axis), (), 0, length) for axis, length in enumerate(array.shape)]
        where[longest] = (where[longest] + shift) % array.shape[longest]
        spots.append(tuple(where))
    return array.at[spots[0]].set(low).at[spots[1]].set(high)


def shard_levels(key, shape, shards, low, high):
    level, own = 1.0, jax.random.fold_in(key, 6)
    for position, parts in shards:
        steps = jnp.exp(jax.random.uniform(jax.random.fold_in(own, position), (parts,), jnp.float32, low / len(shards), high / len(shards)))
        level = level * jnp.repeat(steps, shape[position] // parts).reshape([-1 if axis == position else 1 for axis in range(len(shape))])
    return level


def scatter_about(rng, extent, spread, limit, split=(), kind=jnp.bfloat16):
    values = jax.random.normal(rng, extent, jnp.float32) * spread
    if len(split) > 0:
        values = shard_levels(rng, extent, split, -0.22, 0.18) * values
    return jnp.clip(values, min=-limit, max=limit).astype(kind)


def setup_inputs(seed: int = 0, part: int = 0) -> dict:
    key_list = jax.random.split(jax.random.key(seed), 8)
    part_keys = jax.random.split(jax.random.fold_in(key_list[7], part), 8)
    return {
        "eastern_edge_current": scatter_about(part_keys[0], (DEPTH_LAYERS, GRID_PARALLELS, GRID_MERIDIANS), 0.3, 1.5, ((0, 2), (1, 8)), jnp.float32),
        "northern_edge_current": scatter_about(part_keys[1], (DEPTH_LAYERS, GRID_PARALLELS, GRID_MERIDIANS), 0.3, 1.5, ((0, 2), (1, 8)), jnp.float32),
        "thermal_anomaly": scatter_about(part_keys[2], (DEPTH_LAYERS, GRID_PARALLELS, GRID_MERIDIANS), 1.0, 6.0, ((0, 2), (1, 8)), jnp.float32),
        "prior_warming": jnp.clip(0.5 * jax.random.uniform(part_keys[3], (DEPTH_LAYERS, GRID_PARALLELS, GRID_MERIDIANS), jnp.float32) ** shard_levels(part_keys[3], (DEPTH_LAYERS, GRID_PARALLELS, GRID_MERIDIANS), ((0, 2), (1, 8)), -0.2, 0.2), 0.0, 0.5),
        "solute_fields": scatter_about(part_keys[4], (TR, DEPTH_LAYERS, GRID_PARALLELS, GRID_MERIDIANS), 1.0, 6.0, ((2, 8), (3, 2)), jnp.float32),
        "submerged_layer_count": place_ends(jax.random.randint(part_keys[5], (GRID_PARALLELS, GRID_MERIDIANS), 0, DEPTH_LAYERS + 1), jax.random.fold_in(part_keys[5], 1), 0, DEPTH_LAYERS).astype(jnp.int32),
        "reaction_rates": scatter_about(key_list[6], (TR, TR), TR ** -0.5, 1.25, (), jnp.float32),
    }


def eastern_neighbor(q):
    return jnp.concatenate([q[..., 1:], jnp.zeros_like(q[..., :1])], axis=-1)


def west(q):
    return jnp.concatenate([jnp.zeros_like(q[..., :1]), q[..., :-1]], axis=-1)


def northern_neighbor(q):
    return jnp.concatenate([q[..., 1:, :], jnp.zeros_like(q[..., :1, :])], axis=-2)


def south(q):
    return jnp.concatenate([jnp.zeros_like(q[..., :1, :]), q[..., :-1, :]], axis=-2)


def diffusion_operator(q):
    return eastern_neighbor(q) + west(q) + northern_neighbor(q) + south(q) - 4.0 * q


def reference(eastern_edge_current, northern_edge_current, thermal_anomaly, prior_warming, solute_fields, submerged_layer_count, reaction_rates):
    levels = jnp.arange(DEPTH_LAYERS, dtype=jnp.int32)
    ocean_mask = (levels[:, None, None] < submerged_layer_count[None, :, :]).astype(jnp.float32)
    ocean_mask_eastward = ocean_mask * eastern_neighbor(ocean_mask)
    ocean_mask_poleward = ocean_mask * northern_neighbor(ocean_mask)
    coriolis_parameter = (2.0 * (jnp.arange(GRID_PARALLELS, dtype=jnp.float32) + 0.5) / GRID_PARALLELS - 1.0)[:, None]
    thermal_energy = prior_warming
    eastward_current, poleward_current, seawater_warmth, solute_amount = eastern_edge_current, northern_edge_current, thermal_anomaly, solute_fields
    for step in range(STEPS):
        updated_eastward_flow = ocean_mask_eastward * (eastward_current + 0.1 * diffusion_operator(eastward_current) + 0.3 * coriolis_parameter * poleward_current - 0.2 * (eastern_neighbor(seawater_warmth) - seawater_warmth))
        updated_poleward_flow = ocean_mask_poleward * (poleward_current + 0.1 * diffusion_operator(poleward_current) - 0.3 * coriolis_parameter * eastward_current - 0.2 * (northern_neighbor(seawater_warmth) - seawater_warmth))
        seawater_warmth = ocean_mask * (seawater_warmth + 0.1 * diffusion_operator(seawater_warmth) + 0.5 * thermal_energy)
        eastward_current, poleward_current = updated_eastward_flow, updated_poleward_flow
        flux_x = jnp.maximum(eastward_current, 0.0) * solute_amount + jnp.minimum(eastward_current, 0.0) * eastern_neighbor(solute_amount)
        flux_y = jnp.maximum(poleward_current, 0.0) * solute_amount + jnp.minimum(poleward_current, 0.0) * northern_neighbor(solute_amount)
        advected = solute_amount - 0.5 * ((flux_x - west(flux_x)) + (flux_y - south(flux_y)))
        atten = 0.1 + 0.3 * jnp.maximum(advected[0], 0.0)
        summed = jnp.cumsum(atten, axis=0)
        depth_tau = jnp.concatenate([jnp.zeros_like(atten[:1]), summed[:-1]], axis=0)
        top = jnp.exp(-depth_tau)
        thermal_energy = 2.0 * ocean_mask * (top - jnp.exp(-(depth_tau + atten)))
        react = jnp.einsum("ab,bzyx->azyx", reaction_rates, advected, precision=lax.Precision.HIGHEST)
        solute_amount = ocean_mask * (advected + 0.5 * top * react)
    return eastward_current, poleward_current, seawater_warmth, thermal_energy, solute_amount
```

```python
import functools

import jax
import jax.numpy as jnp
from jax import lax
from jax.experimental import pallas as pl
from jax.experimental.pallas import tpu as pltpu
from jax.sharding import PartitionSpec as P

ROWS = 8
LANES = 128
PAD = 4
EXT = ROWS + 2 * PAD
PAIR = 2
VMEM = 40 * 1024 * 1024
F32 = jnp.float32


def east(q):
    lane = lax.broadcasted_iota(jnp.int32, q.shape, q.ndim - 1)
    return jnp.where(lane < q.shape[-1] - 1, pltpu.roll(q, q.shape[-1] - 1, q.ndim - 1), 0.0)


def west(q):
    lane = lax.broadcasted_iota(jnp.int32, q.shape, q.ndim - 1)
    return jnp.where(lane > 0, pltpu.roll(q, 1, q.ndim - 1), 0.0)


def north(q):
    return pltpu.roll(q, q.shape[-2] - 1, q.ndim - 2)


def south(q):
    return pltpu.roll(q, 1, q.ndim - 2)


def lap(q):
    return east(q) + west(q) + north(q) + south(q) - 4.0 * q


def kernel(
    sizes,
    u_hbm, v_hbm, t_hbm, h_hbm, c_hbm, n_hbm, r_hbm,
    u_out, v_out, t_out, h_out, c_out,
    pk_n, pk_s, rc_n, rc_s, cnt_n, cnt_s, ext, ext_n, t_base, wet_strip,
    c_mid, row_lo, row_hi, col_ed, got_n, got_s, got_w, got_e,
    f_send, f_recv, h_send, h_recv,
    u_in, v_in, t_in, h_in, c_in, n_in, r_in, in_sem,
    d_ssem, d_rsem, c0_ssem, c0_rsem, c1_ssem, c1_rsem, f_ssem, f_rsem, h_ssem, h_rsem,
):
    tracers, depth, share, nlon, nrole, nstrip = sizes
    width = nlon * LANES
    arrays = (
        (u_hbm, u_in), (v_hbm, v_in), (t_hbm, t_in), (h_hbm, h_in), (n_hbm, n_in), (c_hbm, c_in), (r_hbm, r_in),
    )
    loads = [pltpu.make_async_copy(a, b, in_sem.at[i]) for i, (a, b) in enumerate(arrays)]
    for load in loads:
        load.start()
    s = lax.axis_index("lat") * nrole + lax.axis_index("role")
    col = lax.axis_index("lon")
    has_n, has_s = s < nstrip - 1, s > 0
    has_e, has_w = col < nlon - 1, col > 0
    sn, ss = lax.rem(s + 1, nstrip), lax.rem(s + nstrip - 1, nstrip)
    dev_n = {"lat": sn // nrole, "role": lax.rem(sn, nrole)}
    dev_s = {"lat": ss // nrole, "role": lax.rem(ss, nrole)}
    dev_e = {"lon": lax.rem(col + 1, nlon)}
    dev_w = {"lon": lax.rem(col + nlon - 1, nlon)}

    barrier = pltpu.get_barrier_semaphore()

    def greet(dev):
        pl.semaphore_signal(barrier, inc=1, device_id=dev, device_id_type=pl.DeviceIdType.MESH)

    pl.when(has_n)(lambda: greet(dev_n))
    pl.when(has_s)(lambda: greet(dev_s))
    for d in range(1, nlon):
        greet({"lon": lax.rem(col + d, nlon)})

    def copy(src, dst, ssem, rsem, dev):
        return pltpu.make_async_remote_copy(
            src_ref=src, dst_ref=dst, send_sem=ssem, recv_sem=rsem,
            device_id=dev, device_id_type=pl.DeviceIdType.MESH,
        )

    def start(copies):
        for c, send, _ in copies:
            pl.when(send)(c.start)

    def wait_recv(copies):
        for c, _, recv in copies:
            pl.when(recv)(c.wait_recv)

    def wait_send(copies):
        for c, send, _ in copies:
            pl.when(send)(c.wait_send)

    for load in loads[:5]:
        load.wait()
    pk_n[:, 0:3, :] = v_in[:, 5:8, :]
    pk_n[:, 3:5, :] = u_in[:, 6:8, :]
    pk_n[:, 5:7, :] = t_in[:, 6:8, :]
    pk_n[:, 7:8, :] = h_in[:, 7:8, :]
    pk_s[:, 0:2, :] = u_in[:, 0:2, :]
    pk_s[:, 2:4, :] = v_in[:, 0:2, :]
    pk_s[:, 4:6, :] = t_in[:, 0:2, :]
    pk_s[:, 6:7, :] = h_in[:, 0:1, :]
    pk_s[:, 7:8, :] = h_in[:, 0:1, :]

    lane = lax.broadcasted_iota(jnp.int32, (ROWS, LANES), 1)
    row = lax.broadcasted_iota(jnp.int32, (ROWS, LANES), 0)

    def pack(m, k, x):
        row_lo[m, k] = x[:, 0, :]
        row_hi[m, k] = x[:, ROWS - 1, :]
        acc = x[0]
        for t in range(1, tracers):
            here = (lane == 2 * t - 1) | (lane == 2 * t)
            acc = jnp.where(here, pltpu.roll(x[t], 2 * t, 1), acc)
        col_ed[m, k] = acc

    dyn = [
        (copy(pk_n, rc_s, d_ssem.at[0], d_rsem.at[0], dev_n), has_n, has_s),
        (copy(pk_s, rc_n, d_ssem.at[1], d_rsem.at[1], dev_s), has_s, has_n),
        (copy(n_in, cnt_s, d_ssem.at[2], d_rsem.at[2], dev_n), has_n, has_s),
        (copy(n_in, cnt_n, d_ssem.at[3], d_rsem.at[3], dev_s), has_s, has_n),
    ]
    first = [
        (copy(row_hi.at[0], got_s.at[0], c0_ssem.at[0], c0_rsem.at[0], dev_n), has_n, has_s),
        (copy(row_lo.at[0], got_n.at[0], c0_ssem.at[1], c0_rsem.at[1], dev_s), has_s, has_n),
        (copy(col_ed.at[0], got_w.at[0], c0_ssem.at[2], c0_rsem.at[2], dev_e), has_e, has_w),
        (copy(col_ed.at[0], got_e.at[0], c0_ssem.at[3], c0_rsem.at[3], dev_w), has_w, has_e),
    ]

    def second(g):
        two = pl.ds(g * PAIR, PAIR)
        routes = (
            (row_hi, got_s, dev_n, has_n, has_s), (row_lo, got_n, dev_s, has_s, has_n),
            (col_ed, got_w, dev_e, has_e, has_w), (col_ed, got_e, dev_w, has_w, has_e),
        )
        return [
            (copy(a.at[1, two], b.at[1, two], c1_ssem.at[i, g], c1_rsem.at[i, g], dev), send, recv)
            for i, (a, b, dev, send, recv) in enumerate(routes)
        ]

    def faces(m):
        out = []
        for d in range(1, nlon):
            p = lax.rem(col + d, nlon)
            out.append(copy(f_send.at[m, p], f_recv.at[m, col], f_ssem.at[m, d], f_rsem.at[m, d], {"lon": p}))
        return out

    def heats(m):
        out = []
        for d in range(1, nlon):
            p = lax.rem(col + d, nlon)
            out.append(copy(h_send.at[m, p], h_recv.at[m, col], h_ssem.at[m, d], h_rsem.at[m, d], {"lon": p}))
        return out

    pl.semaphore_wait(barrier, nlon - 1 + jnp.minimum(s, 1) + jnp.minimum(nstrip - 1 - s, 1))
    start(dyn)
    for load in loads[5:]:
        load.wait()
    for k in range(depth):
        pack(0, k, c_in[:, k])
    start(first)

    @pl.when(jnp.logical_not(has_s))
    def _():
        rc_s[...] = jnp.zeros_like(rc_s)
        cnt_s[...] = jnp.zeros_like(cnt_s)
        got_s[...] = jnp.zeros_like(got_s)

    @pl.when(jnp.logical_not(has_n))
    def _():
        rc_n[...] = jnp.zeros_like(rc_n)
        cnt_n[...] = jnp.zeros_like(cnt_n)
        got_n[...] = jnp.zeros_like(got_n)

    @pl.when(jnp.logical_not(has_w))
    def _():
        got_w[...] = jnp.zeros_like(got_w)

    @pl.when(jnp.logical_not(has_e))
    def _():
        got_e[...] = jnp.zeros_like(got_e)

    wide = tracers * ROWS
    spread = (
        lax.broadcasted_iota(jnp.int32, (wide, tracers), 0) // ROWS
        == lax.broadcasted_iota(jnp.int32, (wide, tracers), 1)
    ).astype(F32)
    gather = (
        lax.broadcasted_iota(jnp.int32, (tracers, wide), 1) // ROWS
        == lax.broadcasted_iota(jnp.int32, (tracers, wide), 0)
    ).astype(F32)
    exact = lax.Precision.HIGHEST
    rates = jnp.dot(
        spread, jnp.dot(r_in[...], gather, precision=exact, preferred_element_type=F32),
        precision=exact, preferred_element_type=F32,
    )
    same_row = (
        lax.broadcasted_iota(jnp.int32, (wide, wide), 0) % ROWS
        == lax.broadcasted_iota(jnp.int32, (wide, wide), 1) % ROWS
    )
    rates = jnp.where(same_row, rates, 0.0)
    rates_hi = rates.astype(jnp.bfloat16)
    rates_lo = (rates - rates_hi.astype(F32)).astype(jnp.bfloat16)

    zero = jnp.zeros((share, PAD, width), F32)
    for f in range(4):
        ext[f, :, 0:PAD, :] = zero
        ext[f, :, PAD + ROWS :, :] = zero
    ext_n[0:PAD, :] = jnp.zeros((PAD, width), jnp.int32)
    ext_n[PAD + ROWS :, :] = jnp.zeros((PAD, width), jnp.int32)
    for f, ref in enumerate((u_in, v_in, t_in, h_in)):
        ext[f, :, PAD : PAD + ROWS, :] = ref[...]
    ext_n[PAD : PAD + ROWS, :] = n_in[...]

    wait_recv(dyn)
    ext[0, :, 2:4, :] = rc_s[:, 3:5, :]
    ext[1, :, 1:4, :] = rc_s[:, 0:3, :]
    ext[2, :, 2:4, :] = rc_s[:, 5:7, :]
    ext[3, :, 3:4, :] = rc_s[:, 7:8, :]
    ext[0, :, 12:14, :] = rc_n[:, 0:2, :]
    ext[1, :, 12:14, :] = rc_n[:, 2:4, :]
    ext[2, :, 12:14, :] = rc_n[:, 4:6, :]
    ext[3, :, 12:13, :] = rc_n[:, 6:7, :]
    ext_n[2:4, :] = cnt_s[6:8, :]
    ext_n[12:14, :] = cnt_n[0:2, :]

    shape = (share, EXT, width)
    level = col * share + lax.broadcasted_iota(jnp.int32, shape, 0)
    wet = (level < ext_n[...][None]).astype(F32)
    wet_u = wet * east(wet)
    wet_v = wet * north(wet)
    spot = (s * ROWS - PAD + lax.broadcasted_iota(jnp.int32, shape, 1)).astype(F32)
    fcor = 0.3 * (2.0 * (spot + 0.5) / (nstrip * ROWS) - 1.0)

    def advance(u, v, t):
        new_u = wet_u * (u + 0.1 * lap(u) + fcor * v - 0.2 * (east(t) - t))
        new_v = wet_v * (v + 0.1 * lap(v) - fcor * u - 0.2 * (north(t) - t))
        return new_u, new_v

    def publish(m, u, v):
        for p in range(nlon):
            lo = p * LANES
            cols = slice(lo, lo + LANES)
            v_edge = jnp.zeros((ROWS, LANES), F32)
            u_edge = jnp.zeros((ROWS, LANES), F32)
            for l in range(share):
                f_send[m, p, l] = u[l, PAD : PAD + ROWS, cols]
                f_send[m, p, share + l] = v[l, PAD : PAD + ROWS, cols]
                v_edge = jnp.where(row == l, v[l, PAD - 1 : PAD, cols], v_edge)
                if p:
                    u_edge = jnp.where(lane == l, u[l, PAD : PAD + ROWS, lo - 1 : lo], u_edge)
            f_send[m, p, 2 * share] = v_edge
            f_send[m, p, 2 * share + 1] = u_edge
        for c in faces(m):
            c.start()
        f_recv[m, col] = f_send[m, col]

    u0, v0, t0 = ext[0], ext[1], ext[2]
    u1, v1 = advance(u0, v0, t0)
    publish(0, u1, v1)
    t1 = wet * (t0 + 0.1 * lap(t0) + 0.5 * ext[3])
    u2, v2 = advance(u1, v1, t1)
    publish(1, u2, v2)
    u_out[...] = u2[:, PAD : PAD + ROWS, :]
    v_out[...] = v2[:, PAD : PAD + ROWS, :]
    t_base[...] = (wet * (t1 + 0.1 * lap(t1)))[:, PAD : PAD + ROWS, :]
    wet_strip[...] = wet[:, PAD : PAD + ROWS, :]

    depth_here = n_in[:, pl.ds(pl.multiple_of(col * LANES, LANES), LANES)]

    def tile_step(m, source, target):
        coefs, sides, light = {}, {}, {}
        state = [jnp.zeros((ROWS, LANES), F32), jnp.ones((ROWS, LANES), F32)]

        def prepare(k):
            p, l = k // share, k % share
            u = f_recv[m, p, l]
            v = f_recv[m, p, share + l]
            v_s = jnp.where(row == 0, f_recv[m, p, 2 * share, l : l + 1, :], pltpu.roll(v, 1, 0))
            u_w = jnp.where(lane == 0, f_recv[m, p, 2 * share + 1, :, l : l + 1], pltpu.roll(u, 1, 1))
            a_0 = 1.0 - 0.5 * (
                (jnp.maximum(u, 0.0) - jnp.minimum(u_w, 0.0)) + (jnp.maximum(v, 0.0) - jnp.minimum(v_s, 0.0))
            )
            coefs[k] = (
                a_0, -0.5 * jnp.minimum(u, 0.0), 0.5 * jnp.maximum(u_w, 0.0),
                -0.5 * jnp.minimum(v, 0.0), 0.5 * jnp.maximum(v_s, 0.0),
            )
            sides[k] = jnp.where(
                lane % 2 == 0, pltpu.roll(got_w[m, k], 1, 1), pltpu.roll(got_e[m, k], LANES - 1, 1)
            )

        def advect(k, t):
            a_0, a_e, a_w, a_n, a_s = coefs[k]
            x = source[t, k]
            edge = pltpu.roll(sides[k], (LANES - 2 * t) % LANES, 1)
            x_n = jnp.where(row == ROWS - 1, got_n[m, k, t : t + 1, :], pltpu.roll(x, ROWS - 1, 0))
            x_s = jnp.where(row == 0, got_s[m, k, t : t + 1, :], pltpu.roll(x, 1, 0))
            x_e = jnp.where(lane == LANES - 1, edge, pltpu.roll(x, LANES - 1, 1))
            x_w = jnp.where(lane == 0, edge, pltpu.roll(x, 1, 1))
            return a_0 * x + (a_e * x_e + a_w * x_w) + (a_n * x_n + a_s * x_s)

        def shine(k):
            p, l = k // share, k % share
            prepare(k)
            lead = advect(k, 0)
            wet_k = (k < depth_here).astype(F32)
            tau, top = state
            tau = tau + (0.1 + 0.3 * jnp.maximum(lead, 0.0))
            below = jnp.exp(-tau)
            h_send[m, p, l] = 2.0 * wet_k * (top - below)
            light[k] = (lead, wet_k, top)
            state[:] = [tau, below]
            if k == depth - 1:
                for c in heats(m):
                    c.start()
                h_recv[m, col] = h_send[m, col]

        groups = depth // PAIR
        held = {}
        for g in range(groups + 1):
            if g < groups:
                if m:
                    wait_recv(second(g))
                levels = range(g * PAIR, (g + 1) * PAIR)
                for k in levels:
                    shine(k)
                adv = [
                    jnp.concatenate([light[k][0]] + [advect(k, t) for t in range(1, tracers)], axis=0)
                    for k in levels
                ]
                hi = [a.astype(jnp.bfloat16) for a in adv]
                lo = [(a - b.astype(F32)).astype(jnp.bfloat16) for a, b in zip(adv, hi)]
                held[g] = (adv, jnp.concatenate(hi, axis=1), jnp.concatenate(lo, axis=1))
            if g > 0:
                adv, hi, lo = held.pop(g - 1)
                r = (
                    jnp.dot(rates_hi, hi, preferred_element_type=F32)
                    + jnp.dot(rates_hi, lo, preferred_element_type=F32)
                    + jnp.dot(rates_lo, hi, preferred_element_type=F32)
                )
                for n in range(PAIR):
                    k = (g - 1) * PAIR + n
                    _, wet_k, top = light[k]
                    gain = r[:, n * LANES : (n + 1) * LANES].reshape(tracers, ROWS, LANES)
                    new = wet_k * (adv[n].reshape(tracers, ROWS, LANES) + (0.5 * top) * gain)
                    target[:, k] = new
                    if m == 0:
                        pack(1, k, new)
                if m == 0:
                    start(second(g - 1))

    wait_recv(first)
    for c in faces(0):
        c.wait_recv()
    tile_step(0, c_in, c_mid)
    for c in faces(1):
        c.wait_recv()
    tile_step(1, c_mid, c_out)

    for c in heats(0):
        c.wait_recv()
    for p in range(nlon):
        cols = slice(p * LANES, (p + 1) * LANES)
        t_out[:, :, cols] = t_base[:, :, cols] + 0.5 * wet_strip[:, :, cols] * h_recv[0, p]
    wait_send(dyn)
    wait_send(first)
    for g in range(depth // PAIR):
        wait_send(second(g))
    for m in range(2):
        for c in faces(m):
            c.wait_send()
        for c in heats(m):
            c.wait_send()
    for c in heats(1):
        c.wait_recv()
    for p in range(nlon):
        h_out[:, :, p * LANES : (p + 1) * LANES] = h_recv[1, p]


def store(*refs):
    sources, results, sem = refs[:5], refs[5:10], refs[10]
    saves = [pltpu.make_async_copy(a, b, sem.at[i]) for i, (a, b) in enumerate(zip(sources, results))]
    for save in saves:
        save.start()
    for save in saves:
        save.wait()


def shards(sizes, u, v, t, h, c, n, r):
    tracers, depth, share, nlon, _, _ = sizes
    strip = jax.ShapeDtypeStruct(u.shape, F32)
    tile = (ROWS, LANES)
    strip_buf = pltpu.VMEM(u.shape, F32)
    dma = pltpu.SemaphoreType.DMA
    hbm = pl.BlockSpec(memory_space=pltpu.HBM)
    vmem = pl.BlockSpec(memory_space=pltpu.VMEM)
    outs = pl.pallas_call(
        functools.partial(kernel, sizes),
        out_shape=(strip_buf, strip_buf, strip_buf, strip_buf, pltpu.VMEM(c.shape, F32)),
        in_specs=[hbm] * 7,
        out_specs=(vmem,) * 5,
        scratch_shapes=[
            strip_buf, strip_buf, strip_buf, strip_buf,
            pltpu.VMEM(n.shape, jnp.int32), pltpu.VMEM(n.shape, jnp.int32),
            pltpu.VMEM((4, share, EXT, u.shape[2]), F32),
            pltpu.VMEM((EXT, u.shape[2]), jnp.int32),
            strip_buf, strip_buf,
            pltpu.VMEM(c.shape, F32),
            pltpu.VMEM((2, depth, tracers, LANES), F32),
            pltpu.VMEM((2, depth, tracers, LANES), F32),
            pltpu.VMEM((2, depth) + tile, F32),
            pltpu.VMEM((2, depth, tracers, LANES), F32),
            pltpu.VMEM((2, depth, tracers, LANES), F32),
            pltpu.VMEM((2, depth) + tile, F32),
            pltpu.VMEM((2, depth) + tile, F32),
            pltpu.VMEM((2, nlon, 2 * share + 2) + tile, F32),
            pltpu.VMEM((2, nlon, 2 * share + 2) + tile, F32),
            pltpu.VMEM((2, nlon, share) + tile, F32),
            pltpu.VMEM((2, nlon, share) + tile, F32),
            strip_buf, strip_buf, strip_buf, strip_buf, pltpu.VMEM(c.shape, F32),
            pltpu.VMEM(n.shape, jnp.int32), pltpu.VMEM(r.shape, F32), dma((7,)),
            dma((4,)), dma((4,)), dma((4,)), dma((4,)),
            dma((4, depth)), dma((4, depth)),
            dma((2, nlon)), dma((2, nlon)), dma((2, nlon)), dma((2, nlon)),
        ],
        compiler_params=pltpu.CompilerParams(
            collective_id=0, has_side_effects=True, vmem_limit_bytes=VMEM
        ),
    )(*(pltpu.with_memory_space_constraint(x, pltpu.HBM) for x in (u, v, t, h, c, n, r)))
    return pl.pallas_call(
        store,
        out_shape=(strip, strip, strip, strip, jax.ShapeDtypeStruct(c.shape, F32)),
        in_specs=[vmem] * 5,
        out_specs=(hbm,) * 5,
        scratch_shapes=[dma((5,))],
        compiler_params=pltpu.CompilerParams(vmem_limit_bytes=VMEM),
    )(*outs)


def solution(mesh):
    nlon, nrole = mesh.shape["lon"], mesh.shape["role"]
    nstrip = mesh.shape["lat"] * nrole
    strip = P("lon", ("grp", "lat", "role"), None)
    tile = P(None, None, ("grp", "lat", "role"), "lon")

    def run(u, v, t, h, c, n, r):
        sizes = (c.shape[0], c.shape[1], u.shape[0] // nlon, nlon, nrole, nstrip)
        return jax.shard_map(
            functools.partial(shards, sizes),
            mesh=mesh,
            in_specs=(strip, strip, strip, strip, tile, P(("grp", "lat", "role"), None), P()),
            out_specs=(strip, strip, strip, strip, tile),
            check_vma=False,
        )(u, v, t, h, c, n, r)

    return run
```

```python
import functools

import jax
import jax.numpy as jnp
from jax import lax
from jax.experimental import pallas as pl
from jax.experimental.pallas import tpu as pltpu
from jax.sharding import PartitionSpec as P

ROWS = 8
LANES = 128
EXT = 2 * ROWS
WIDE = 2 * LANES
PAIR = 2
STEP = 4
GROUP = 8
VMEM = 40 * 1024 * 1024
F32 = jnp.float32
EXACT = lax.Precision.HIGHEST


def east(q):
    return pltpu.roll(q, q.shape[-1] - 1, q.ndim - 1)


def west(q):
    return pltpu.roll(q, 1, q.ndim - 1)


def north(q):
    return pltpu.roll(q, q.shape[-2] - 1, q.ndim - 2)


def south(q):
    return pltpu.roll(q, 1, q.ndim - 2)


def lap(q):
    return east(q) + west(q) + north(q) + south(q) - 4.0 * q


def upwind(u, u_w, v, v_s):
    u_neg, v_neg = jnp.minimum(u, 0.0), jnp.minimum(v, 0.0)
    uw_pos, vs_pos = jnp.maximum(u_w, 0.0), jnp.maximum(v_s, 0.0)
    a_0 = 1.0 - 0.5 * (
        (jnp.maximum(u, 0.0) - jnp.minimum(u_w, 0.0)) + (jnp.maximum(v, 0.0) - jnp.minimum(v_s, 0.0))
    )
    return a_0, -0.5 * u_neg, 0.5 * uw_pos, -0.5 * v_neg, 0.5 * vs_pos


def mix(a, x, x_e, x_w, x_n, x_s):
    return a[0] * x + (a[1] * x_e + a[2] * x_w) + (a[3] * x_n + a[4] * x_s)


def split(a):
    hi = a.astype(jnp.bfloat16)
    return hi, (a - hi.astype(F32)).astype(jnp.bfloat16)


def product(a, b):
    a_hi, a_lo = a
    b_hi, b_lo = b
    return (
        jnp.dot(a_hi, b_hi, preferred_element_type=F32)
        + jnp.dot(a_hi, b_lo, preferred_element_type=F32)
        + jnp.dot(a_lo, b_hi, preferred_element_type=F32)
    )


def kernel(
    sizes,
    u_hbm, v_hbm, t_hbm, h_hbm, c_hbm, n_hbm, r_hbm,
    out, c_out,
    strips, ext, edge_s, edge_x, cnt, c_in, c_mid, row_n, row_s, ring_n, ring_s,
    col_ed, got_e, got_w, cor, ring_c, cex, cec, cf1, t_base, o_send, r_in, in_sem,
    x_ss, x_rs, hx_ss, hx_rs, n_ss, n_rs, s_ss, s_rs, ex_ss, ex_rs, en_ss, en_rs, es_ss, es_rs,
    k_ss, k_rs, c_ss, c_rs, q_ss, q_rs, uv_ss, uv_rs, t_ss, t_rs, h_ss, h_rs,
):
    tracers, depth, share, nlon, nrole, nstrip = sizes
    loads = [pltpu.make_async_copy(a, strips.at[i], in_sem.at[i]) for i, a in enumerate((u_hbm, v_hbm, t_hbm, h_hbm))]
    loads.append(pltpu.make_async_copy(n_hbm, cnt.at[0:ROWS], in_sem.at[4]))
    loads.append(pltpu.make_async_copy(c_hbm, c_in, in_sem.at[5]))
    loads.append(pltpu.make_async_copy(r_hbm, r_in, in_sem.at[6]))
    for load in loads:
        load.start()

    s = lax.axis_index("lat") * nrole + lax.axis_index("role")
    col = lax.axis_index("lon")
    has_n, has_s = s < nstrip - 1, s > 0
    has_e, has_w = col < nlon - 1, col > 0
    sn, ss = lax.rem(s + 1, nstrip), lax.rem(s + nstrip - 1, nstrip)
    to_n = {"lat": sn // nrole, "role": lax.rem(sn, nrole)}
    to_s = {"lat": ss // nrole, "role": lax.rem(ss, nrole)}
    lon_e, lon_w = lax.rem(col + 1, nlon), lax.rem(col + nlon - 1, nlon)

    def others(first):
        return [(d, lax.rem(col + d, nlon)) for d in range(first, nlon)]

    barrier = pltpu.get_barrier_semaphore()

    def greet(dev):
        pl.semaphore_signal(barrier, inc=1, device_id=dev, device_id_type=pl.DeviceIdType.MESH)

    for d, p in others(1):
        greet({"lon": p})

    @pl.when(has_n)
    def _():
        for d, p in others(0):
            greet(dict(to_n, lon=p))

    @pl.when(has_s)
    def _():
        for d, p in others(0):
            greet(dict(to_s, lon=p))

    def copy(src, dst, ssem, rsem, dev):
        return pltpu.make_async_remote_copy(
            src_ref=src, dst_ref=dst, send_sem=ssem, recv_sem=rsem,
            device_id=dev, device_id_type=pl.DeviceIdType.MESH,
        )

    def start(cond, copies):
        if cond is None:
            for c in copies:
                c.start()
        else:
            pl.when(cond)(lambda: start(None, copies))

    def wait_recv(cond, copies):
        if cond is None:
            for c in copies:
                c.wait_recv()
        else:
            pl.when(cond)(lambda: wait_recv(None, copies))

    def wait_send(cond, copies):
        if cond is None:
            for c in copies:
                c.wait_send()
        else:
            pl.when(cond)(lambda: wait_send(None, copies))

    def cols(p):
        return pl.ds(pl.multiple_of(p * LANES, LANES), LANES)

    main = pl.ds(0, LANES)
    mine = pl.ds(col * share, share)
    x_main = [
        copy(strips.at[0:3, :, :, cols(p)], ext.at[0:3, mine, 0:ROWS, main], x_ss.at[d], x_rs.at[d], {"lon": p})
        for d, p in others(1)
    ]
    x_heat = [
        copy(strips.at[3, :, :, cols(p)], ext.at[3, mine, 0:ROWS, main], hx_ss.at[d], hx_rs.at[d], {"lon": p})
        for d, p in others(1)
    ]
    rows_n = [
        copy(
            strips.at[:, :, 5:8, cols(p)], ext.at[:, mine, 13:16, main], n_ss.at[d], n_rs.at[d], dict(to_n, lon=p)
        )
        for d, p in others(0)
    ]
    rows_s = [
        copy(
            strips.at[:, :, 0:2, cols(p)], ext.at[:, mine, 8:10, main], s_ss.at[d], s_rs.at[d], dict(to_s, lon=p)
        )
        for d, p in others(0)
    ]
    edges_x = [
        copy(edge_s.at[p], edge_x.at[col, 0:ROWS], ex_ss.at[d], ex_rs.at[d], {"lon": p}) for d, p in others(1)
    ]
    edges_n = [
        copy(edge_s.at[p, 5:8], edge_x.at[col, 13:16], en_ss.at[d], en_rs.at[d], dict(to_n, lon=p))
        for d, p in others(0)
    ]
    edges_s = [
        copy(edge_s.at[p, 0:2], edge_x.at[col, 8:10], es_ss.at[d], es_rs.at[d], dict(to_s, lon=p))
        for d, p in others(0)
    ]
    depth_n = [copy(n_hbm.at[6:8], cnt.at[14:16], k_ss.at[0], k_rs.at[0], to_n)]
    depth_s = [copy(n_hbm.at[0:2], cnt.at[8:10], k_ss.at[1], k_rs.at[1], to_s)]
    near_n = [copy(c_hbm.at[:, :, 7, :], row_s.at[0], c_ss.at[0], c_rs.at[0], to_n)]
    near_s = [copy(c_hbm.at[:, :, 0, :], row_n.at[0], c_ss.at[1], c_rs.at[1], to_s)]
    far_n = [copy(c_hbm.at[:, :, 6, :], row_s.at[1], c_ss.at[2], c_rs.at[2], to_n)]
    far_s = [copy(c_hbm.at[:, :, 1, :], row_n.at[1], c_ss.at[3], c_rs.at[3], to_s)]
    edge_e = [copy(col_ed, got_w, c_ss.at[4], c_rs.at[4], {"lon": lon_e})]
    edge_w = [copy(col_ed, got_e, c_ss.at[5], c_rs.at[5], {"lon": lon_w})]
    corners = [
        (copy(col_ed.at[:, 7, :], cor.at[1, 1], q_ss.at[0], q_rs.at[0], dict(to_n, lon=lon_e)), has_n & has_e, has_s & has_w),
        (copy(col_ed.at[:, 7, :], cor.at[1, 0], q_ss.at[1], q_rs.at[1], dict(to_n, lon=lon_w)), has_n & has_w, has_s & has_e),
        (copy(col_ed.at[:, 0, :], cor.at[0, 1], q_ss.at[2], q_rs.at[2], dict(to_s, lon=lon_e)), has_s & has_e, has_n & has_w),
        (copy(col_ed.at[:, 0, :], cor.at[0, 0], q_ss.at[3], q_rs.at[3], dict(to_s, lon=lon_w)), has_s & has_w, has_n & has_e),
    ]
    flow_out = [
        copy(o_send.at[0:2, pl.ds(p * share, share)], out.at[0:2, :, :, cols(col)], uv_ss.at[d], uv_rs.at[d], {"lon": p})
        for d, p in others(1)
    ]
    warm_out = [
        copy(o_send.at[2, pl.ds(p * share, share)], out.at[2, :, :, cols(col)], t_ss.at[d], t_rs.at[d], {"lon": p})
        for d, p in others(1)
    ]
    heat_out = [
        copy(o_send.at[3, pl.ds(p * share, share)], out.at[3, :, :, cols(col)], h_ss.at[d], h_rs.at[d], {"lon": p})
        for d, p in others(1)
    ]

    lane = lax.broadcasted_iota(jnp.int32, (ROWS, LANES), 1)
    row = lax.broadcasted_iota(jnp.int32, (ROWS, LANES), 0)
    eastern, western = lane % STEP == 0, lane % STEP == STEP - 1

    for load in loads[:4]:
        load.wait()
    for p in range(nlon):
        acc = jnp.zeros((ROWS, LANES), F32)
        for f in range(4):
            for l in range(share):
                g = GROUP * (f * share + l)
                e = strips[f, l, :, (p + 1) * LANES : (p + 2) * LANES] if p < nlon - 1 else jnp.zeros((ROWS, LANES), F32)
                w = strips[f, l, :, (p - 1) * LANES : p * LANES] if p > 0 else jnp.zeros((ROWS, LANES), F32)
                both = jnp.where(lane < LANES // 2, e, w)
                acc = jnp.where((lane + (3 + LANES - g)) % LANES < 5, pltpu.roll(both, g, 1), acc)
        edge_s[p] = acc

    pl.semaphore_wait(barrier, nlon - 1 + nlon * (jnp.minimum(s, 1) + jnp.minimum(nstrip - 1 - s, 1)))
    start(None, x_main)
    start(has_n, rows_n + edges_n + depth_n)
    start(has_s, rows_s + edges_s + depth_s)
    start(None, edges_x + x_heat)
    start(has_n, near_n)
    start(has_s, near_s)

    loads[5].wait()
    for k in range(depth):
        acc = c_in[0, k]
        for t in range(1, tracers):
            here = (lane >= STEP * t - 2) & (lane < STEP * t + 2)
            acc = jnp.where(here, pltpu.roll(c_in[t, k], STEP * t, 1), acc)
        col_ed[k] = acc
    start(has_e, edge_e)
    start(has_w, edge_w)
    for c, send, _ in corners:
        start(send, [c])
    start(has_n, far_n)
    start(has_s, far_s)

    @pl.when(jnp.logical_not(has_s))
    def _():
        ext[:, :, 13:16, 0:LANES] = jnp.zeros((4, depth, 3, LANES), F32)
        edge_x[:, 13:16, :] = jnp.zeros((nlon, 3, LANES), F32)
        cnt[14:16, :] = jnp.zeros((2, nlon * LANES), jnp.int32)
        row_s[...] = jnp.zeros_like(row_s)

    @pl.when(jnp.logical_not(has_n))
    def _():
        ext[:, :, 8:10, 0:LANES] = jnp.zeros((4, depth, 2, LANES), F32)
        edge_x[:, 8:10, :] = jnp.zeros((nlon, 2, LANES), F32)
        cnt[8:10, :] = jnp.zeros((2, nlon * LANES), jnp.int32)
        row_n[...] = jnp.zeros_like(row_n)

    @pl.when(jnp.logical_not(has_w))
    def _():
        got_w[...] = jnp.zeros_like(got_w)

    @pl.when(jnp.logical_not(has_e))
    def _():
        got_e[...] = jnp.zeros_like(got_e)

    for i, there in enumerate((has_n, has_s)):
        for j, beside in enumerate((has_e, has_w)):

            @pl.when(jnp.logical_not(there & beside))
            def _(i=i, j=j):
                cor[i, j] = jnp.zeros((depth, LANES), F32)

    loads[4].wait()
    loads[6].wait()
    for f in range(4):
        ext[f, mine, 0:ROWS, 0:LANES] = strips[f, :, :, cols(col)]
    edge_x[col, 0:ROWS] = edge_s[col]

    high = tracers * ROWS
    spread = (
        lax.broadcasted_iota(jnp.int32, (high, tracers), 0) // ROWS
        == lax.broadcasted_iota(jnp.int32, (high, tracers), 1)
    ).astype(F32)
    gather = (
        lax.broadcasted_iota(jnp.int32, (tracers, high), 1) // ROWS
        == lax.broadcasted_iota(jnp.int32, (tracers, high), 0)
    ).astype(F32)
    rates = jnp.dot(
        spread, jnp.dot(r_in[...], gather, precision=EXACT, preferred_element_type=F32),
        precision=EXACT, preferred_element_type=F32,
    )
    same_row = (
        lax.broadcasted_iota(jnp.int32, (high, high), 0) % ROWS
        == lax.broadcasted_iota(jnp.int32, (high, high), 1) % ROWS
    )
    rates = split(jnp.where(same_row, rates, 0.0))
    spot0 = lax.broadcasted_iota(jnp.int32, (LANES, tracers), 0)
    pick0 = ((spot0 + 1) % LANES // STEP == lax.broadcasted_iota(jnp.int32, (LANES, tracers), 1)).astype(F32)
    spot1 = lax.broadcasted_iota(jnp.int32, (tracers, LANES), 1)
    pick1 = ((spot1 + 1) % LANES // STEP == lax.broadcasted_iota(jnp.int32, (tracers, LANES), 0)).astype(F32)
    across = jnp.dot(
        lax.dot_general(
            pick0, r_in[...], (((1,), (1,)), ((), ())), precision=EXACT, preferred_element_type=F32
        ),
        pick1, precision=EXACT, preferred_element_type=F32,
    )
    side_a = lax.broadcasted_iota(jnp.int32, (LANES, LANES), 0) % STEP
    side_b = lax.broadcasted_iota(jnp.int32, (LANES, LANES), 1) % STEP
    across = split(jnp.where((side_a == side_b) & ((side_a == 0) | (side_a == STEP - 1)), across, 0.0))

    wait_recv(has_s, rows_n + edges_n + depth_n)
    wait_recv(has_n, rows_s + edges_s + depth_s)
    wait_recv(None, x_main + edges_x + x_heat)

    lane2 = lax.broadcasted_iota(jnp.int32, (EXT, LANES), 1)
    window = (lane2 < 2) | (lane2 >= LANES - 3)
    for q in range(nlon):
        held = edge_x[q]
        for f in range(4):
            for l in range(share):
                g = GROUP * (f * share + l)
                moved = pltpu.roll(held, (LANES - g) % LANES, 1) if g else held
                ext[f, q * share + l, :, LANES:WIDE] = jnp.where(window, moved, 0.0)
    wet_e = jnp.where((lane2 < 2) & has_e, cnt[:, cols(lon_e)], 0)
    wet_w = jnp.where((lane2 >= LANES - 3) & has_w, cnt[:, cols(lon_w)], 0)
    n_main = cnt[:, cols(col)]
    n_side = jnp.where(lane2 < LANES // 2, wet_e, wet_w)
    layers = jnp.concatenate([n_main, n_side], axis=1)
    level_main = n_main[0:ROWS]

    line = lax.broadcasted_iota(jnp.int32, (EXT, WIDE), 0)
    spot = (s * ROWS + jnp.where(line < 12, line, line - EXT)).astype(F32)
    fcor = 0.3 * (2.0 * (spot + 0.5) / (nstrip * ROWS) - 1.0)

    for k in range(depth):
        wet = (k < layers).astype(F32)
        wet_u = wet * east(wet)
        wet_v = wet * north(wet)

        def advance(u, v, t):
            new_u = wet_u * (u + 0.1 * lap(u) + fcor * v - 0.2 * (east(t) - t))
            new_v = wet_v * (v + 0.1 * lap(v) - fcor * u - 0.2 * (north(t) - t))
            return new_u, new_v

        u0, v0, t0, h0 = ext[0, k], ext[1, k], ext[2, k], ext[3, k]
        u1, v1 = advance(u0, v0, t0)
        for i, a in enumerate(upwind(u1, west(u1), v1, south(v1))):
            cex[i, k] = a[:, 0:LANES]
            cec[i, k] = a[0:ROWS, LANES:WIDE]
        t1 = wet * (t0 + 0.1 * lap(t0) + 0.5 * h0)
        u2, v2 = advance(u1, v1, t1)
        u_here, v_here = u2[0:ROWS, 0:LANES], v2[0:ROWS, 0:LANES]
        u_back, v_back = west(u2)[0:ROWS, 0:LANES], south(v2)[0:ROWS, 0:LANES]
        for i, a in enumerate(upwind(u_here, u_back, v_here, v_back)):
            cf1[i, k] = a
        t_base[k] = (wet * (t1 + 0.1 * lap(t1)))[0:ROWS, 0:LANES]
        o_send[0, k] = u_here
        o_send[1, k] = v_here
    start(None, flow_out)
    out[0:2, :, :, cols(col)] = o_send[0:2, mine]

    def sides_of(x):
        return jnp.where(eastern, pltpu.roll(x, 1, 1), pltpu.roll(x, LANES - 1, 1))

    def tile_step(m, source, target, above, below, beside):
        def coefs(k):
            if m == 0:
                return [cex[i, k, 0:ROWS, :] for i in range(5)]
            return [cf1[i, k] for i in range(5)]

        def advect(k, t, a, side):
            x = source[t, k]
            edge = pltpu.roll(side, (LANES - STEP * t) % LANES, 1)
            x_n = jnp.where(row == ROWS - 1, above(t, k), pltpu.roll(x, ROWS - 1, 0))
            x_s = jnp.where(row == 0, below(t, k), pltpu.roll(x, 1, 0))
            x_e = jnp.where(lane == LANES - 1, edge, pltpu.roll(x, LANES - 1, 1))
            x_w = jnp.where(lane == 0, edge, pltpu.roll(x, 1, 1))
            return mix(a, x, x_e, x_w, x_n, x_s)

        light, state = {}, [jnp.zeros((ROWS, LANES), F32), jnp.ones((ROWS, LANES), F32)]

        def shine(k):
            lead = advect(k, 0, coefs(k), sides_of(beside(k)))
            wet_k = (k < level_main).astype(F32)
            tau, top = state
            tau = tau + (0.1 + 0.3 * jnp.maximum(lead, 0.0))
            under = jnp.exp(-tau)
            heat = 2.0 * wet_k * (top - under)
            if m == 0:
                o_send[2, k] = t_base[k] + 0.5 * wet_k * heat
            else:
                o_send[3, k] = heat
            light[k] = (lead, wet_k, top)
            state[:] = [tau, under]
            if k == depth - 1:
                start(None, warm_out if m == 0 else heat_out)
                out[2 + m, :, :, cols(col)] = o_send[2 + m, mine]

        groups = depth // PAIR
        held = {}
        if m:
            for k in range(depth):
                shine(k)
        for g in range(groups + 1):
            if g < groups:
                levels = range(g * PAIR, (g + 1) * PAIR)
                adv = []
                for k in levels:
                    if m == 0:
                        shine(k)
                    a, side = coefs(k), sides_of(beside(k))
                    adv.append(
                        jnp.concatenate([light[k][0]] + [advect(k, t, a, side) for t in range(1, tracers)], axis=0)
                    )
                parts = [split(a) for a in adv]
                held[g] = (
                    adv, (jnp.concatenate([a for a, _ in parts], axis=1), jnp.concatenate([b for _, b in parts], axis=1))
                )
            if g > 0:
                adv, both = held.pop(g - 1)
                r = product(rates, both)
                for n in range(PAIR):
                    k = (g - 1) * PAIR + n
                    _, wet_k, top = light[k]
                    gain = r[:, n * LANES : (n + 1) * LANES].reshape(tracers, ROWS, LANES)
                    target[:, k] = wet_k * (adv[n].reshape(tracers, ROWS, LANES) + (0.5 * top) * gain)

    def sideways(k):
        return jnp.where(lane % STEP < 2, got_e[k], got_w[k])

    def ring_rows():
        adv, tops = [], []
        for i in range(2):
            rows, line_at, inner = (row_n, 8, 7) if i == 0 else (row_s, 15, 0)
            a = [cex[j, :, line_at, :] for j in range(5)]
            corner = sides_of(jnp.where(lane % STEP < 2, cor[i, 0], cor[i, 1]))
            values = []
            for t in range(tracers):
                x, far, near = rows[0, t], rows[1, t], c_in[t, :, inner, :]
                edge = pltpu.roll(corner, (LANES - STEP * t) % LANES, 1)
                x_e = jnp.where(lane == LANES - 1, edge, pltpu.roll(x, LANES - 1, 1))
                x_w = jnp.where(lane == 0, edge, pltpu.roll(x, 1, 1))
                x_n, x_s = (far, near) if i == 0 else (near, far)
                values.append(mix(a, x, x_e, x_w, x_n, x_s))
            tau = 0.1 + 0.3 * jnp.maximum(values[0], 0.0)
            tau = jnp.where(row > 0, pltpu.roll(tau, 1, 0), 0.0)
            for shift in (1, 2, 4):
                tau = tau + jnp.where(row >= shift, pltpu.roll(tau, shift, 0), 0.0)
            tops.append(jnp.exp(-tau))
            adv.append(jnp.concatenate(values, axis=0))
        parts = [split(a) for a in adv]
        r = product(
            rates, (jnp.concatenate([a for a, _ in parts], axis=1), jnp.concatenate([b for _, b in parts], axis=1))
        )
        for i, (ring, line_at) in enumerate(((ring_n, 8), (ring_s, 15))):
            wet = (row < n_main[line_at : line_at + 1, :]).astype(F32)
            gain = r[:, i * LANES : (i + 1) * LANES].reshape(tracers, ROWS, LANES)
            ring[...] = wet * (adv[i].reshape(tracers, ROWS, LANES) + (0.5 * tops[i]) * gain)

    def ring_cols():
        def both(x):
            return jnp.where(
                eastern, jnp.broadcast_to(x[:, 0:1], x.shape), jnp.broadcast_to(x[:, LANES - 1 :], x.shape)
            )

        edge_n = jnp.where(lane % STEP < 2, cor[0, 0], cor[0, 1])
        edge_s = jnp.where(lane % STEP < 2, cor[1, 0], cor[1, 1])
        wet_n = both(n_side[0:ROWS])
        tau = jnp.zeros((ROWS, LANES), F32)
        values, tops = [], []
        for k in range(depth):
            x, own = sideways(k), col_ed[k]
            a = [both(cec[i, k]) for i in range(5)]
            x_e = pltpu.roll(jnp.where(eastern, own, x), LANES - 1, 1)
            x_w = pltpu.roll(jnp.where(western, own, x), 1, 1)
            x_n = jnp.where(row == ROWS - 1, edge_n[k : k + 1, :], pltpu.roll(x, ROWS - 1, 0))
            x_s = jnp.where(row == 0, edge_s[k : k + 1, :], pltpu.roll(x, 1, 0))
            value = mix(a, x, x_e, x_w, x_n, x_s)
            values.append(value)
            tops.append(jnp.exp(-tau))
            tau = tau + (0.1 + 0.3 * jnp.maximum(both(value), 0.0))
        r = product(split(jnp.concatenate(values, axis=0)), across)
        for k in range(depth):
            wet = (k < wet_n).astype(F32)
            ring_c[k] = wet * (values[k] + (0.5 * tops[k]) * r[k * ROWS : (k + 1) * ROWS])

    wait_recv(has_s, near_n)
    wait_recv(has_n, near_s)
    wait_recv(has_w, edge_e)
    wait_recv(has_e, edge_w)
    tile_step(
        0, c_in, c_mid,
        lambda t, k: row_n[0, t, k : k + 1, :], lambda t, k: row_s[0, t, k : k + 1, :], sideways,
    )
    wait_recv(has_s, far_n)
    wait_recv(has_n, far_s)
    for c, _, recv in corners:
        wait_recv(recv, [c])
    ring_rows()
    ring_cols()
    tile_step(
        1, c_mid, c_out,
        lambda t, k: ring_n[t, k : k + 1, :], lambda t, k: ring_s[t, k : k + 1, :], lambda k: ring_c[k],
    )

    wait_send(None, x_main + x_heat + edges_x)
    wait_send(has_n, rows_n + edges_n + depth_n + near_n + far_n)
    wait_send(has_s, rows_s + edges_s + depth_s + near_s + far_s)
    wait_send(has_e, edge_e)
    wait_send(has_w, edge_w)
    for c, send, _ in corners:
        wait_send(send, [c])
    wait_send(None, flow_out + warm_out)
    wait_recv(None, flow_out + warm_out)
    wait_send(None, heat_out)
    wait_recv(None, heat_out)


def store(out, c_out, u_dst, v_dst, t_dst, h_dst, c_dst, sem):
    saves = [pltpu.make_async_copy(c_out, c_dst, sem.at[4])]
    saves += [pltpu.make_async_copy(out.at[i], b, sem.at[i]) for i, b in enumerate((u_dst, v_dst, t_dst, h_dst))]
    for save in saves:
        save.start()
    for save in saves:
        save.wait()


def shards(sizes, u, v, t, h, c, n, r):
    tracers, depth, share, nlon, _, _ = sizes
    width = nlon * LANES
    strip = jax.ShapeDtypeStruct(u.shape, F32)
    tile = (ROWS, LANES)
    dma = pltpu.SemaphoreType.DMA
    hbm = pl.BlockSpec(memory_space=pltpu.HBM)
    vmem = pl.BlockSpec(memory_space=pltpu.VMEM)
    buf = pltpu.VMEM
    line = (tracers, depth, LANES)
    pair = [dma((nlon,)), dma((nlon,))]
    held = pl.pallas_call(
        functools.partial(kernel, sizes),
        out_shape=(buf((4, share, ROWS, width), F32), buf(c.shape, F32)),
        in_specs=[hbm] * 7,
        out_specs=(vmem, vmem),
        scratch_shapes=[
            buf((4, share, ROWS, width), F32),
            buf((4, depth, EXT, WIDE), F32),
            buf((nlon,) + tile, F32),
            buf((nlon, EXT, LANES), F32),
            buf((EXT, width), jnp.int32),
            buf(c.shape, F32), buf(c.shape, F32),
            buf((2,) + line, F32), buf((2,) + line, F32), buf(line, F32), buf(line, F32),
            buf((depth,) + tile, F32), buf((depth,) + tile, F32), buf((depth,) + tile, F32),
            buf((2, 2, depth, LANES), F32),
            buf((depth,) + tile, F32),
            buf((5, depth, EXT, LANES), F32),
            buf((5, depth) + tile, F32),
            buf((5, depth) + tile, F32),
            buf((depth,) + tile, F32),
            buf((4, depth) + tile, F32),
            buf(r.shape, F32),
            dma((7,)),
            *(pair * 7),
            dma((2,)), dma((2,)), dma((6,)), dma((6,)), dma((4,)), dma((4,)),
            *(pair * 3),
        ],
        compiler_params=pltpu.CompilerParams(
            collective_id=0, has_side_effects=True, vmem_limit_bytes=VMEM
        ),
    )(*(pltpu.with_memory_space_constraint(x, pltpu.HBM) for x in (u, v, t, h, c, n, r)))
    return pl.pallas_call(
        store,
        out_shape=(strip, strip, strip, strip, jax.ShapeDtypeStruct(c.shape, F32)),
        in_specs=[vmem] * 2,
        out_specs=(hbm,) * 5,
        scratch_shapes=[dma((5,))],
        compiler_params=pltpu.CompilerParams(vmem_limit_bytes=VMEM),
    )(*held)


def solution(mesh):
    nlon, nrole = mesh.shape["lon"], mesh.shape["role"]
    nstrip = mesh.shape["lat"] * nrole
    strip = P("lon", ("grp", "lat", "role"), None)
    tile = P(None, None, ("grp", "lat", "role"), "lon")

    def run(u, v, t, h, c, n, r):
        sizes = (c.shape[0], c.shape[1], u.shape[0] // nlon, nlon, nrole, nstrip)
        return jax.shard_map(
            functools.partial(shards, sizes),
            mesh=mesh,
            in_specs=(strip, strip, strip, strip, tile, P(("grp", "lat", "role"), None), P()),
            out_specs=(strip, strip, strip, strip, tile),
            check_vma=False,
        )(u, v, t, h, c, n, r)

    return run
```

```python
import functools

import jax
import jax.numpy as jnp
from jax import lax
from jax.experimental import pallas as pl
from jax.experimental.pallas import tpu as pltpu
from jax.sharding import PartitionSpec as P

ROWS = 8
LANES = 128
EXT = 2 * ROWS
WIDE = 2 * LANES
PAIR = 2
STEP = 4
GROUP = 8
VMEM = 40 * 1024 * 1024
F32 = jnp.float32
EXACT = lax.Precision.HIGHEST


def east(q):
    return pltpu.roll(q, q.shape[-1] - 1, q.ndim - 1)


def west(q):
    return pltpu.roll(q, 1, q.ndim - 1)


def north(q):
    return pltpu.roll(q, q.shape[-2] - 1, q.ndim - 2)


def south(q):
    return pltpu.roll(q, 1, q.ndim - 2)


def lap(q):
    return east(q) + west(q) + north(q) + south(q) - 4.0 * q


def upwind(u, u_w, v, v_s):
    u_neg, v_neg = jnp.minimum(u, 0.0), jnp.minimum(v, 0.0)
    uw_pos, vs_pos = jnp.maximum(u_w, 0.0), jnp.maximum(v_s, 0.0)
    a_0 = 1.0 - 0.5 * (
        (jnp.maximum(u, 0.0) - jnp.minimum(u_w, 0.0)) + (jnp.maximum(v, 0.0) - jnp.minimum(v_s, 0.0))
    )
    return a_0, -0.5 * u_neg, 0.5 * uw_pos, -0.5 * v_neg, 0.5 * vs_pos


def mix(a, x, x_e, x_w, x_n, x_s):
    return a[0] * x + (a[1] * x_e + a[2] * x_w) + (a[3] * x_n + a[4] * x_s)


def split(a):
    hi = a.astype(jnp.bfloat16)
    return hi, (a - hi.astype(F32)).astype(jnp.bfloat16)


def halves(a):
    return jnp.concatenate(split(a), axis=1)


def product(a, b):
    a_hi, a_lo = a
    b_hi, b_lo = b
    return (
        jnp.dot(a_hi, b_hi, preferred_element_type=F32)
        + jnp.dot(a_hi, b_lo, preferred_element_type=F32)
        + jnp.dot(a_lo, b_hi, preferred_element_type=F32)
    )


def kernel(
    sizes,
    u_hbm, v_hbm, t_hbm, h_hbm, c_hbm, n_hbm, r_hbm,
    out, c_out,
    stage, tall, flow, cnt, c_in, c_raw, c_mid, row_n, row_s, raw_n, raw_s, ring_n, ring_s,
    col_ed, got_e, got_w, cor, ring_c, lead_c, lead_n, lead_s, cex, cec, cf1, t_base, o_send, r_in, in_sem, strip_sem,
    x_ss, x_rs, hx_ss, hx_rs, n_ss, n_rs, s_ss, s_rs,
    k_ss, k_rs, c_ss, c_rs, q_ss, q_rs, uv_ss, uv_rs, t_ss, t_rs, h_ss, h_rs,
):
    tracers, depth, share, nlon, nrole, nstrip = sizes
    early = 3 * share + 1

    def slot(f, l):
        return f * share + l + (f == 3)

    strip_loads = [
        pltpu.make_async_copy(
            a.at[:, :, p * LANES : (p + 1) * LANES], stage.at[p, slot(f, 0) : slot(f, 0) + share], strip_sem.at[f, p]
        )
        for f, a in enumerate((u_hbm, v_hbm, t_hbm, h_hbm))
        for p in range(nlon)
    ]
    loads = [
        pltpu.make_async_copy(a, b, in_sem.at[i])
        for i, (a, b) in enumerate(((n_hbm, cnt.at[0:ROWS]), (c_hbm, c_in), (r_hbm, r_in)))
    ]
    for load in strip_loads + loads:
        load.start()

    s = lax.axis_index("lat") * nrole + lax.axis_index("role")
    col = lax.axis_index("lon")
    has_n, has_s = s < nstrip - 1, s > 0
    has_e, has_w = col < nlon - 1, col > 0
    sn, ss = lax.rem(s + 1, nstrip), lax.rem(s + nstrip - 1, nstrip)
    to_n = {"lat": sn // nrole, "role": lax.rem(sn, nrole)}
    to_s = {"lat": ss // nrole, "role": lax.rem(ss, nrole)}
    lon_e, lon_w = lax.rem(col + 1, nlon), lax.rem(col + nlon - 1, nlon)

    def others(first):
        return [(d, lax.rem(col + d, nlon)) for d in range(first, nlon)]

    barrier = pltpu.get_barrier_semaphore()

    def greet(dev):
        pl.semaphore_signal(barrier, inc=1, device_id=dev, device_id_type=pl.DeviceIdType.MESH)

    for d, p in others(1):
        greet({"lon": p})

    @pl.when(has_n)
    def _():
        for d, p in others(0):
            greet(dict(to_n, lon=p))

    @pl.when(has_s)
    def _():
        for d, p in others(0):
            greet(dict(to_s, lon=p))

    def copy(src, dst, ssem, rsem, dev):
        return pltpu.make_async_remote_copy(
            src_ref=src, dst_ref=dst, send_sem=ssem, recv_sem=rsem,
            device_id=dev, device_id_type=pl.DeviceIdType.MESH,
        )

    def start(cond, copies):
        if cond is None:
            for c in copies:
                c.start()
        else:
            pl.when(cond)(lambda: start(None, copies))

    def wait_recv(cond, copies):
        if cond is None:
            for c in copies:
                c.wait_recv()
        else:
            pl.when(cond)(lambda: wait_recv(None, copies))

    def wait_send(cond, copies):
        if cond is None:
            for c in copies:
                c.wait_send()
        else:
            pl.when(cond)(lambda: wait_send(None, copies))

    def cols(p):
        return pl.ds(pl.multiple_of(p * LANES, LANES), LANES)

    mine = pl.ds(col * share, share)
    x_main = [
        copy(stage.at[p, 0:early], tall.at[col, 0:early, 0:ROWS], x_ss.at[d], x_rs.at[d], {"lon": p})
        for d, p in others(1)
    ]
    x_heat = [
        copy(
            stage.at[p, early : early + share], tall.at[col, early : early + share, 0:ROWS],
            hx_ss.at[d], hx_rs.at[d], {"lon": p},
        )
        for d, p in others(1)
    ]
    rows_n = [
        copy(stage.at[p, :, 5:8], tall.at[col, :, 13:16], n_ss.at[d], n_rs.at[d], dict(to_n, lon=p))
        for d, p in others(0)
    ]
    rows_s = [
        copy(stage.at[p, :, 0:2], tall.at[col, :, 8:10], s_ss.at[d], s_rs.at[d], dict(to_s, lon=p))
        for d, p in others(0)
    ]
    depth_n = [copy(n_hbm.at[6:8], cnt.at[14:16], k_ss.at[0], k_rs.at[0], to_n)]
    depth_s = [copy(n_hbm.at[0:2], cnt.at[8:10], k_ss.at[1], k_rs.at[1], to_s)]
    near_n = [copy(c_hbm.at[:, :, 7, :], row_s.at[0], c_ss.at[0], c_rs.at[0], to_n)]
    near_s = [copy(c_hbm.at[:, :, 0, :], row_n.at[0], c_ss.at[1], c_rs.at[1], to_s)]
    far_n = [copy(c_hbm.at[:, :, 6, :], row_s.at[1], c_ss.at[2], c_rs.at[2], to_n)]
    far_s = [copy(c_hbm.at[:, :, 1, :], row_n.at[1], c_ss.at[3], c_rs.at[3], to_s)]
    edge_e = [copy(col_ed, got_w, c_ss.at[4], c_rs.at[4], {"lon": lon_e})]
    edge_w = [copy(col_ed, got_e, c_ss.at[5], c_rs.at[5], {"lon": lon_w})]
    corners = [
        (copy(col_ed.at[:, 7, :], cor.at[1, 1], q_ss.at[0], q_rs.at[0], dict(to_n, lon=lon_e)), has_n & has_e, has_s & has_w),
        (copy(col_ed.at[:, 7, :], cor.at[1, 0], q_ss.at[1], q_rs.at[1], dict(to_n, lon=lon_w)), has_n & has_w, has_s & has_e),
        (copy(col_ed.at[:, 0, :], cor.at[0, 1], q_ss.at[2], q_rs.at[2], dict(to_s, lon=lon_e)), has_s & has_e, has_n & has_w),
        (copy(col_ed.at[:, 0, :], cor.at[0, 0], q_ss.at[3], q_rs.at[3], dict(to_s, lon=lon_w)), has_s & has_w, has_n & has_e),
    ]
    flow_out = [
        copy(o_send.at[0:2, pl.ds(p * share, share)], out.at[0:2, :, :, cols(col)], uv_ss.at[d], uv_rs.at[d], {"lon": p})
        for d, p in others(1)
    ]
    warm_out = [
        copy(o_send.at[2, pl.ds(p * share, share)], out.at[2, :, :, cols(col)], t_ss.at[d], t_rs.at[d], {"lon": p})
        for d, p in others(1)
    ]
    heat_out = [
        copy(o_send.at[3, pl.ds(p * share, share)], out.at[3, :, :, cols(col)], h_ss.at[d], h_rs.at[d], {"lon": p})
        for d, p in others(1)
    ]

    lane = lax.broadcasted_iota(jnp.int32, (ROWS, LANES), 1)
    row = lax.broadcasted_iota(jnp.int32, (ROWS, LANES), 0)
    eastern, western = lane % STEP == 0, lane % STEP == STEP - 1

    def spots(axis):
        return lax.broadcasted_iota(jnp.int32, (LANES, LANES), axis)

    def twice(mask):
        one = mask.astype(F32).astype(jnp.bfloat16)
        return jnp.concatenate([one, one], axis=0)

    far_lane = (spots(1) + STEP // 2) % STEP
    take = twice(spots(0) == (far_lane + LANES - STEP // 2) % LANES)
    give = twice(
        ((spots(0) % STEP == 0) & (spots(1) == LANES - 1)) | ((spots(0) % STEP == STEP - 1) & (spots(1) == 0))
    )

    def unpack(a, b):
        parts = halves(jnp.concatenate([a, b], axis=0))
        place = lax.broadcasted_iota(jnp.int32, (1, WIDE), 1) % LANES
        only = [
            ((place + 1) % LANES // STEP == t).astype(F32).astype(jnp.bfloat16) for t in range(tracers)
        ]
        e = jnp.dot(jnp.concatenate([parts * o for o in only], axis=0), give, preferred_element_type=F32)
        return [[e[(2 * t + i) * ROWS : (2 * t + i + 1) * ROWS] for i in range(2)] for t in range(tracers)]

    for load in strip_loads:
        load.wait()
    blank = jnp.zeros((ROWS, LANES), F32)
    for p in range(nlon):
        acc = blank
        for f in range(4):
            for l in range(share):
                g = GROUP * (f * share + l)
                e = stage[p + 1, slot(f, l)] if p < nlon - 1 else blank
                w = stage[p - 1, slot(f, l)] if p > 0 else blank
                both = jnp.where(lane < LANES // 2, e, w)
                acc = jnp.where((lane + (3 + LANES - g)) % LANES < 5, pltpu.roll(both, g, 1), acc)
        stage[p, 3 * share] = acc

    pl.semaphore_wait(barrier, nlon - 1 + nlon * (jnp.minimum(s, 1) + jnp.minimum(nstrip - 1 - s, 1)))
    start(has_n, rows_n[::-1] + depth_n)
    start(has_s, rows_s[::-1] + depth_s)
    start(None, x_main)
    start(has_n, near_n)
    start(has_s, near_s)
    start(None, x_heat)

    loads[1].wait()
    for k in range(depth):
        picked = jnp.dot(
            jnp.concatenate([halves(c_in[t, k]) for t in range(tracers)], axis=0), take, preferred_element_type=F32
        )
        acc = picked[0:ROWS]
        for t in range(1, tracers):
            here = (lane >= STEP * t - 2) & (lane < STEP * t + 2)
            acc = jnp.where(here, picked[t * ROWS : (t + 1) * ROWS], acc)
        col_ed[k] = acc
    start(has_e, edge_e)
    start(has_w, edge_w)
    for c, send, _ in corners:
        start(send, [c])
    start(has_n, far_n)
    start(has_s, far_s)

    @pl.when(jnp.logical_not(has_s))
    def _():
        tall[:, :, 13:16, :] = jnp.zeros((nlon, 4 * share + 1, 3, LANES), F32)
        cnt[14:16, :] = jnp.zeros((2, nlon * LANES), jnp.int32)
        row_s[...] = jnp.zeros_like(row_s)

    @pl.when(jnp.logical_not(has_n))
    def _():
        tall[:, :, 8:10, :] = jnp.zeros((nlon, 4 * share + 1, 2, LANES), F32)
        cnt[8:10, :] = jnp.zeros((2, nlon * LANES), jnp.int32)
        row_n[...] = jnp.zeros_like(row_n)

    @pl.when(jnp.logical_not(has_w))
    def _():
        got_w[...] = jnp.zeros_like(got_w)

    @pl.when(jnp.logical_not(has_e))
    def _():
        got_e[...] = jnp.zeros_like(got_e)

    for i, there in enumerate((has_n, has_s)):
        for j, beside in enumerate((has_e, has_w)):

            @pl.when(jnp.logical_not(there & beside))
            def _(i=i, j=j):
                cor[i, j] = jnp.zeros((depth, LANES), F32)

    loads[0].wait()
    loads[2].wait()
    tall[col, :, 0:ROWS] = stage[col]
    lead_rates = [jnp.broadcast_to(r_in[0:1, b : b + 1], (ROWS, LANES)) for b in range(tracers)]

    high = tracers * ROWS
    spread = (
        lax.broadcasted_iota(jnp.int32, (high, tracers), 0) // ROWS
        == lax.broadcasted_iota(jnp.int32, (high, tracers), 1)
    ).astype(F32)
    gather = (
        lax.broadcasted_iota(jnp.int32, (tracers, high), 1) // ROWS
        == lax.broadcasted_iota(jnp.int32, (tracers, high), 0)
    ).astype(F32)
    rates = jnp.dot(
        spread, jnp.dot(r_in[...], gather, precision=EXACT, preferred_element_type=F32),
        precision=EXACT, preferred_element_type=F32,
    )
    same_row = (
        lax.broadcasted_iota(jnp.int32, (high, high), 0) % ROWS
        == lax.broadcasted_iota(jnp.int32, (high, high), 1) % ROWS
    )
    rates = split(jnp.where(same_row, rates, 0.0))
    spot0 = lax.broadcasted_iota(jnp.int32, (LANES, tracers), 0)
    pick0 = ((spot0 + 1) % LANES // STEP == lax.broadcasted_iota(jnp.int32, (LANES, tracers), 1)).astype(F32)
    spot1 = lax.broadcasted_iota(jnp.int32, (tracers, LANES), 1)
    pick1 = ((spot1 + 1) % LANES // STEP == lax.broadcasted_iota(jnp.int32, (tracers, LANES), 0)).astype(F32)
    across = jnp.dot(
        lax.dot_general(
            pick0, r_in[...], (((1,), (1,)), ((), ())), precision=EXACT, preferred_element_type=F32
        ),
        pick1, precision=EXACT, preferred_element_type=F32,
    )
    side_a = lax.broadcasted_iota(jnp.int32, (LANES, LANES), 0) % STEP
    side_b = lax.broadcasted_iota(jnp.int32, (LANES, LANES), 1) % STEP
    across = split(jnp.where((side_a == side_b) & ((side_a == 0) | (side_a == STEP - 1)), across, 0.0))

    wait_recv(has_s, rows_n + depth_n)
    wait_recv(has_n, rows_s + depth_s)
    wait_recv(None, x_main)

    lane2 = lax.broadcasted_iota(jnp.int32, (EXT, LANES), 1)
    window = (lane2 < 2) | (lane2 >= LANES - 3)

    def field(f, k):
        q, l = k // share, k % share
        g = GROUP * (f * share + l)
        held = tall[q, 3 * share]
        moved = pltpu.roll(held, (LANES - g) % LANES, 1) if g else held
        return jnp.concatenate([tall[q, slot(f, l)], jnp.where(window, moved, 0.0)], axis=1)

    wet_e = jnp.where((lane2 < 2) & has_e, cnt[:, cols(lon_e)], 0)
    wet_w = jnp.where((lane2 >= LANES - 3) & has_w, cnt[:, cols(lon_w)], 0)
    n_main = cnt[:, cols(col)]
    n_side = jnp.where(lane2 < LANES // 2, wet_e, wet_w)
    layers = jnp.concatenate([n_main, n_side], axis=1)
    level_main = n_main[0:ROWS]

    line = lax.broadcasted_iota(jnp.int32, (EXT, WIDE), 0)
    spot = (s * ROWS + jnp.where(line < 12, line, line - EXT)).astype(F32)
    fcor = 0.3 * (2.0 * (spot + 0.5) / (nstrip * ROWS) - 1.0)

    def masks(k):
        wet = (k < layers).astype(F32)
        return wet, wet * east(wet), wet * north(wet)

    def advance(m, u, v, t):
        new_u = m[1] * (u + 0.1 * lap(u) + fcor * v - 0.2 * (east(t) - t))
        new_v = m[2] * (v + 0.1 * lap(v) - fcor * u - 0.2 * (north(t) - t))
        return new_u, new_v

    for k in range(depth):
        u1, v1 = advance(masks(k), field(0, k), field(1, k), field(2, k))
        flow[0, k], flow[1, k] = u1, v1
        for i, a in enumerate(upwind(u1, west(u1), v1, south(v1))):
            cex[i, k] = a[:, 0:LANES]
            cec[i, k] = a[0:ROWS, LANES:WIDE]
    wait_recv(None, x_heat)
    for k in range(depth):
        m = masks(k)
        t0 = field(2, k)
        t1 = m[0] * (t0 + 0.1 * lap(t0) + 0.5 * field(3, k))
        u2, v2 = advance(m, flow[0, k], flow[1, k], t1)
        u_here, v_here = u2[0:ROWS, 0:LANES], v2[0:ROWS, 0:LANES]
        u_back, v_back = west(u2)[0:ROWS, 0:LANES], south(v2)[0:ROWS, 0:LANES]
        for i, a in enumerate(upwind(u_here, u_back, v_here, v_back)):
            cf1[i, k] = a
        t_base[k] = (m[0] * (t1 + 0.1 * lap(t1)))[0:ROWS, 0:LANES]
        o_send[0, k] = u_here
        o_send[1, k] = v_here
    start(None, flow_out)
    out[0:2, :, :, cols(col)] = o_send[0:2, mine]

    def coefs(m, k):
        if m == 0:
            return [cex[i, k, 0:ROWS, :] for i in range(5)]
        return [cf1[i, k] for i in range(5)]

    def advect(a, x, edge, above, below):
        x_n = jnp.where(row == ROWS - 1, above, pltpu.roll(x, ROWS - 1, 0))
        x_s = jnp.where(row == 0, below, pltpu.roll(x, 1, 0))
        x_e = jnp.where(lane == LANES - 1, edge, pltpu.roll(x, LANES - 1, 1))
        x_w = jnp.where(lane == 0, edge, pltpu.roll(x, 1, 1))
        return mix(a, x, x_e, x_w, x_n, x_s)

    def lead_of(values):
        parts = [v * a for v, a in zip(values, lead_rates)]
        while len(parts) > 1:
            parts = [sum(parts[i : i + 2]) for i in range(0, len(parts), 2)]
        return parts[0]

    def shine(m, leads):
        tau, top = jnp.zeros((ROWS, LANES), F32), jnp.ones((ROWS, LANES), F32)
        tops = []
        for k, lead in enumerate(leads):
            wet_k = (k < level_main).astype(F32)
            tau = tau + (0.1 + 0.3 * jnp.maximum(lead, 0.0))
            under = jnp.exp(-tau)
            heat = 2.0 * wet_k * (top - under)
            if m == 0:
                o_send[2, k] = t_base[k] + 0.5 * wet_k * heat
            else:
                o_send[3, k] = heat
            tops.append(top)
            top = under
        start(None, heat_out if m else warm_out)
        out[2 + m, :, :, cols(col)] = o_send[2 + m, mine]
        return tops

    def react(blocks):
        parts = [split(a) for a in blocks]
        r = product(
            rates, (jnp.concatenate([a for a, _ in parts], axis=1), jnp.concatenate([b for _, b in parts], axis=1))
        )
        return [r[:, i * LANES : (i + 1) * LANES].reshape(tracers, ROWS, LANES) for i in range(len(blocks))]

    def settle(k, top, value, gain):
        return (k < level_main).astype(F32) * (value + (0.5 * top) * gain)

    def sideways(k):
        return jnp.where(lane % STEP < 2, got_e[k], got_w[k])

    def ring_rows():
        tops, wets = [], []
        ends = unpack(*(jnp.where(lane % STEP < 2, cor[i, 0], cor[i, 1]) for i in range(2)))
        for i in range(2):
            rows, line_at, inner = (row_n, 8, 7) if i == 0 else (row_s, 15, 0)
            a = [cex[j, :, line_at, :] for j in range(5)]
            values = []
            for t in range(tracers):
                x, far, near = rows[0, t], rows[1, t], c_in[t, :, inner, :]
                edge = ends[t][i]
                x_e = jnp.where(lane == LANES - 1, edge, pltpu.roll(x, LANES - 1, 1))
                x_w = jnp.where(lane == 0, edge, pltpu.roll(x, 1, 1))
                x_n, x_s = (far, near) if i == 0 else (near, far)
                values.append(mix(a, x, x_e, x_w, x_n, x_s))
                (raw_n, raw_s)[i][t] = values[t]
            tau = 0.1 + 0.3 * jnp.maximum(values[0], 0.0)
            tau = jnp.where(row > 0, pltpu.roll(tau, 1, 0), 0.0)
            for shift in (1, 2, 4):
                tau = tau + jnp.where(row >= shift, pltpu.roll(tau, shift, 0), 0.0)
            top = jnp.exp(-tau)
            wet = (row < n_main[line_at : line_at + 1, :]).astype(F32)
            (lead_n, lead_s)[i][...] = wet * (values[0] + (0.5 * top) * lead_of(values))
            tops.append(top)
            wets.append(wet)
        return tops, wets

    def ring_finish(tops, wets):
        blocks = [a[...] for a in (raw_n, raw_s)]
        gains = react([a.reshape(high, LANES) for a in blocks])
        for i, ring in enumerate((ring_n, ring_s)):
            ring[...] = wets[i] * (blocks[i] + (0.5 * tops[i]) * gains[i])

    def ring_cols():
        def both(x):
            return jnp.where(
                eastern, jnp.broadcast_to(x[:, 0:1], x.shape), jnp.broadcast_to(x[:, LANES - 1 :], x.shape)
            )

        edge_n = jnp.where(lane % STEP < 2, cor[0, 0], cor[0, 1])
        edge_s = jnp.where(lane % STEP < 2, cor[1, 0], cor[1, 1])
        wet_n = both(n_side[0:ROWS])
        tau = jnp.zeros((ROWS, LANES), F32)
        values, tops = [], []
        for k in range(depth):
            x, own = sideways(k), col_ed[k]
            a = [both(cec[i, k]) for i in range(5)]
            x_e = pltpu.roll(jnp.where(eastern, own, x), LANES - 1, 1)
            x_w = pltpu.roll(jnp.where(western, own, x), 1, 1)
            x_n = jnp.where(row == ROWS - 1, edge_n[k : k + 1, :], pltpu.roll(x, ROWS - 1, 0))
            x_s = jnp.where(row == 0, edge_s[k : k + 1, :], pltpu.roll(x, 1, 0))
            value = mix(a, x, x_e, x_w, x_n, x_s)
            values.append(value)
            tops.append(jnp.exp(-tau))
            tau = tau + (0.1 + 0.3 * jnp.maximum(both(value), 0.0))
        r = product(split(jnp.concatenate(values, axis=0)), across)
        for k in range(depth):
            wet = (k < wet_n).astype(F32)
            ring_c[k] = wet * (values[k] + (0.5 * tops[k]) * r[k * ROWS : (k + 1) * ROWS])

    groups = [range(g, g + PAIR) for g in range(0, depth, PAIR)]
    wait_recv(has_s, near_n)
    wait_recv(has_n, near_s)
    wait_recv(has_w, edge_e)
    wait_recv(has_e, edge_w)
    leads, firsts = [], []
    for levels in groups:
        edges = unpack(*(sideways(k) for k in levels))
        for i, k in enumerate(levels):
            a = coefs(0, k)
            values = [
                advect(a, c_in[t, k], edges[t][i], row_n[0, t, k : k + 1, :], row_s[0, t, k : k + 1, :])
                for t in range(tracers)
            ]
            for t in range(tracers):
                c_raw[t, k] = values[t]
            leads.append(values[0])
            firsts.append(lead_of(values))
    tops = shine(0, leads)
    for k in range(depth):
        lead_c[k] = settle(k, tops[k], leads[k], firsts[k])

    wait_recv(has_s, far_n)
    wait_recv(has_n, far_s)
    for c, _, recv in corners:
        wait_recv(recv, [c])
    ring_cols()
    ring_light = ring_rows()
    leads = []
    for k in range(depth):
        x, beside = lead_c[k], ring_c[k]
        x_n = jnp.where(row == ROWS - 1, lead_n[k : k + 1, :], pltpu.roll(x, ROWS - 1, 0))
        x_s = jnp.where(row == 0, lead_s[k : k + 1, :], pltpu.roll(x, 1, 0))
        x_e = pltpu.roll(jnp.where(lane == 0, beside, x), LANES - 1, 1)
        x_w = pltpu.roll(jnp.where(lane == LANES - 1, beside, x), 1, 1)
        leads.append(mix(coefs(1, k), x, x_e, x_w, x_n, x_s))
    last = shine(1, leads)

    ring_finish(*ring_light)
    for levels in groups:
        blocks = [c_raw[:, k] for k in levels]
        gains = react([b.reshape(high, LANES) for b in blocks])
        for k, block, gain in zip(levels, blocks, gains):
            c_mid[:, k] = settle(k, tops[k], block, gain)
    for levels in groups:
        edges = unpack(*(ring_c[k] for k in levels))
        blocks = []
        for i, k in enumerate(levels):
            a = coefs(1, k)
            blocks.append(jnp.concatenate([leads[k]] + [
                advect(a, c_mid[t, k], edges[t][i], ring_n[t, k : k + 1, :], ring_s[t, k : k + 1, :])
                for t in range(1, tracers)
            ], axis=0))
        gains = react(blocks)
        for k, block, gain in zip(levels, blocks, gains):
            c_out[:, k] = settle(k, last[k], block.reshape(tracers, ROWS, LANES), gain)

    wait_send(None, x_main + x_heat)
    wait_send(has_n, rows_n + depth_n + near_n + far_n)
    wait_send(has_s, rows_s + depth_s + near_s + far_s)
    wait_send(has_e, edge_e)
    wait_send(has_w, edge_w)
    for c, send, _ in corners:
        wait_send(send, [c])
    wait_send(None, flow_out + warm_out)
    wait_recv(None, flow_out + warm_out)
    wait_send(None, heat_out)
    wait_recv(None, heat_out)


def store(out, c_out, u_dst, v_dst, t_dst, h_dst, c_dst, sem):
    saves = [pltpu.make_async_copy(c_out, c_dst, sem.at[4])]
    saves += [pltpu.make_async_copy(out.at[i], b, sem.at[i]) for i, b in enumerate((u_dst, v_dst, t_dst, h_dst))]
    for save in saves:
        save.start()
    for save in saves:
        save.wait()


def shards(sizes, u, v, t, h, c, n, r):
    tracers, depth, share, nlon, _, _ = sizes
    width = nlon * LANES
    strip = jax.ShapeDtypeStruct(u.shape, F32)
    tile = (ROWS, LANES)
    dma = pltpu.SemaphoreType.DMA
    hbm = pl.BlockSpec(memory_space=pltpu.HBM)
    vmem = pl.BlockSpec(memory_space=pltpu.VMEM)
    buf = pltpu.VMEM
    line = (tracers, depth, LANES)
    pair = [dma((nlon,)), dma((nlon,))]
    held = pl.pallas_call(
        functools.partial(kernel, sizes),
        out_shape=(buf((4, share, ROWS, width), F32), buf(c.shape, F32)),
        in_specs=[hbm] * 7,
        out_specs=(vmem, vmem),
        scratch_shapes=[
            buf((nlon, 4 * share + 1) + tile, F32),
            buf((nlon, 4 * share + 1, EXT, LANES), F32),
            buf((2, depth, EXT, WIDE), F32),
            buf((EXT, width), jnp.int32),
            buf(c.shape, F32), buf(c.shape, F32), buf(c.shape, F32),
            buf((2,) + line, F32), buf((2,) + line, F32),
            buf(line, F32), buf(line, F32), buf(line, F32), buf(line, F32),
            buf((depth,) + tile, F32), buf((depth,) + tile, F32), buf((depth,) + tile, F32),
            buf((2, 2, depth, LANES), F32),
            buf((depth,) + tile, F32), buf((depth,) + tile, F32), buf((depth, LANES), F32), buf((depth, LANES), F32),
            buf((5, depth, EXT, LANES), F32),
            buf((5, depth) + tile, F32),
            buf((5, depth) + tile, F32),
            buf((depth,) + tile, F32),
            buf((4, depth) + tile, F32),
            buf(r.shape, F32),
            dma((3,)), dma((4, nlon)),
            *(pair * 4),
            dma((2,)), dma((2,)), dma((6,)), dma((6,)), dma((4,)), dma((4,)),
            *(pair * 3),
        ],
        compiler_params=pltpu.CompilerParams(
            collective_id=0, has_side_effects=True, vmem_limit_bytes=VMEM
        ),
    )(*(pltpu.with_memory_space_constraint(x, pltpu.HBM) for x in (u, v, t, h, c, n, r)))
    return pl.pallas_call(
        store,
        out_shape=(strip, strip, strip, strip, jax.ShapeDtypeStruct(c.shape, F32)),
        in_specs=[vmem] * 2,
        out_specs=(hbm,) * 5,
        scratch_shapes=[dma((5,))],
        compiler_params=pltpu.CompilerParams(vmem_limit_bytes=VMEM),
    )(*held)


def solution(mesh):
    nlon, nrole = mesh.shape["lon"], mesh.shape["role"]
    nstrip = mesh.shape["lat"] * nrole
    strip = P("lon", ("grp", "lat", "role"), None)
    tile = P(None, None, ("grp", "lat", "role"), "lon")

    def run(u, v, t, h, c, n, r):
        sizes = (c.shape[0], c.shape[1], u.shape[0] // nlon, nlon, nrole, nstrip)
        return jax.shard_map(
            functools.partial(shards, sizes),
            mesh=mesh,
            in_specs=(strip, strip, strip, strip, tile, P(("grp", "lat", "role"), None), P()),
            out_specs=(strip, strip, strip, strip, tile),
            check_vma=False,
        )(u, v, t, h, c, n, r)

    return run
```

```python
import functools

import jax
import jax.numpy as jnp
from jax import lax
from jax.experimental import pallas as pl
from jax.experimental.pallas import tpu as pltpu
from jax.sharding import PartitionSpec as P

ROWS = 8
LANES = 128
EXT = 2 * ROWS
WIDE = 2 * LANES
PAIR = 2
STEP = 4
GROUP = 8
VMEM = 40 * 1024 * 1024
F32 = jnp.float32
EXACT = lax.Precision.HIGHEST


def east(q):
    return pltpu.roll(q, q.shape[-1] - 1, q.ndim - 1)


def west(q):
    return pltpu.roll(q, 1, q.ndim - 1)


def north(q):
    return pltpu.roll(q, q.shape[-2] - 1, q.ndim - 2)


def south(q):
    return pltpu.roll(q, 1, q.ndim - 2)


def lap(q):
    return east(q) + west(q) + north(q) + south(q) - 4.0 * q


def upwind(u, u_w, v, v_s):
    u_neg, v_neg = jnp.minimum(u, 0.0), jnp.minimum(v, 0.0)
    uw_pos, vs_pos = jnp.maximum(u_w, 0.0), jnp.maximum(v_s, 0.0)
    a_0 = 1.0 - 0.5 * (
        (jnp.maximum(u, 0.0) - jnp.minimum(u_w, 0.0)) + (jnp.maximum(v, 0.0) - jnp.minimum(v_s, 0.0))
    )
    return a_0, -0.5 * u_neg, 0.5 * uw_pos, -0.5 * v_neg, 0.5 * vs_pos


def mix(a, x, x_e, x_w, x_n, x_s):
    return a[0] * x + (a[1] * x_e + a[2] * x_w) + (a[3] * x_n + a[4] * x_s)


def split(a):
    hi = a.astype(jnp.bfloat16)
    return hi, (a - hi.astype(F32)).astype(jnp.bfloat16)


def halves(a):
    return jnp.concatenate(split(a), axis=1)


def product(a, b):
    a_hi, a_lo = a
    b_hi, b_lo = b
    return (
        jnp.dot(a_hi, b_hi, preferred_element_type=F32)
        + jnp.dot(a_hi, b_lo, preferred_element_type=F32)
        + jnp.dot(a_lo, b_hi, preferred_element_type=F32)
    )


def kernel(
    sizes,
    u_hbm, v_hbm, t_hbm, h_hbm, c_hbm, n_hbm, r_hbm,
    out, c_out,
    stage, tall, flow, cnt, c_in, c_raw, c_mid, row_n, row_s, raw_n, raw_s, ring_n, ring_s,
    col_ed, send_e, send_w, got_e, got_w, cor, ring_c, lead_c, lead_n, lead_s, cex, cec, cf1, t_base, o_send, r_in, in_sem, strip_sem,
    x_ss, x_rs, n_ss, n_rs, s_ss, s_rs,
    k_ss, k_rs, c_ss, c_rs, q_ss, q_rs, uv_ss, uv_rs, t_ss, t_rs, h_ss, h_rs,
):
    tracers, depth, share, nlon, nrole, nstrip = sizes
    def slot(f, l):
        return f * share + l + (f == 3)

    strip_loads = [
        pltpu.make_async_copy(
            a.at[:, :, p * LANES : (p + 1) * LANES], stage.at[p, slot(f, 0) : slot(f, 0) + share], strip_sem.at[f, p]
        )
        for f, a in enumerate((u_hbm, v_hbm, t_hbm, h_hbm))
        for p in range(nlon)
    ]
    loads = [
        pltpu.make_async_copy(a, b, in_sem.at[i])
        for i, (a, b) in enumerate(((n_hbm, cnt.at[0:ROWS]), (c_hbm, c_in), (r_hbm, r_in)))
    ]
    for load in strip_loads + loads:
        load.start()

    s = lax.axis_index("lat") * nrole + lax.axis_index("role")
    col = lax.axis_index("lon")
    has_n, has_s = s < nstrip - 1, s > 0
    has_e, has_w = col < nlon - 1, col > 0
    sn, ss = lax.rem(s + 1, nstrip), lax.rem(s + nstrip - 1, nstrip)
    to_n = {"lat": sn // nrole, "role": lax.rem(sn, nrole)}
    to_s = {"lat": ss // nrole, "role": lax.rem(ss, nrole)}
    lon_e, lon_w = lax.rem(col + 1, nlon), lax.rem(col + nlon - 1, nlon)

    def others(first):
        return [(d, lax.rem(col + d, nlon)) for d in range(first, nlon)]

    barrier = pltpu.get_barrier_semaphore()

    def greet(dev):
        pl.semaphore_signal(barrier, inc=1, device_id=dev, device_id_type=pl.DeviceIdType.MESH)

    for d, p in others(1):
        greet({"lon": p})

    @pl.when(has_n)
    def _():
        for d, p in others(0):
            greet(dict(to_n, lon=p))

    @pl.when(has_s)
    def _():
        for d, p in others(0):
            greet(dict(to_s, lon=p))

    def copy(src, dst, ssem, rsem, dev):
        return pltpu.make_async_remote_copy(
            src_ref=src, dst_ref=dst, send_sem=ssem, recv_sem=rsem,
            device_id=dev, device_id_type=pl.DeviceIdType.MESH,
        )

    def start(cond, copies):
        if cond is None:
            for c in copies:
                c.start()
        else:
            pl.when(cond)(lambda: start(None, copies))

    def wait_recv(cond, copies):
        if cond is None:
            for c in copies:
                c.wait_recv()
        else:
            pl.when(cond)(lambda: wait_recv(None, copies))

    def wait_send(cond, copies):
        if cond is None:
            for c in copies:
                c.wait_send()
        else:
            pl.when(cond)(lambda: wait_send(None, copies))

    def cols(p):
        return pl.ds(pl.multiple_of(p * LANES, LANES), LANES)

    mine = pl.ds(col * share, share)
    x_main = [
        copy(stage.at[p], tall.at[col, :, 0:ROWS], x_ss.at[d], x_rs.at[d], {"lon": p})
        for d, p in others(1)
    ]
    rows_n = [
        copy(stage.at[p, :, 5:8], tall.at[col, :, 13:16], n_ss.at[d], n_rs.at[d], dict(to_n, lon=p))
        for d, p in others(0)
    ]
    rows_s = [
        copy(stage.at[p, :, 0:2], tall.at[col, :, 8:10], s_ss.at[d], s_rs.at[d], dict(to_s, lon=p))
        for d, p in others(0)
    ]
    depth_n = [copy(n_hbm.at[6:8], cnt.at[14:16], k_ss.at[0], k_rs.at[0], to_n)]
    depth_s = [copy(n_hbm.at[0:2], cnt.at[8:10], k_ss.at[1], k_rs.at[1], to_s)]
    near_n = [copy(c_hbm.at[:, :, 7, :], row_s.at[0], c_ss.at[0], c_rs.at[0], to_n)]
    near_s = [copy(c_hbm.at[:, :, 0, :], row_n.at[0], c_ss.at[1], c_rs.at[1], to_s)]
    far_n = [copy(c_hbm.at[:, :, 6, :], row_s.at[1], c_ss.at[2], c_rs.at[2], to_n)]
    far_s = [copy(c_hbm.at[:, :, 1, :], row_n.at[1], c_ss.at[3], c_rs.at[3], to_s)]
    edge_e = [copy(send_e, got_w, c_ss.at[4], c_rs.at[4], {"lon": lon_e})]
    edge_w = [copy(send_w, got_e, c_ss.at[5], c_rs.at[5], {"lon": lon_w})]
    corners = [
        (copy(col_ed.at[:, 7, :], cor.at[1, 1], q_ss.at[0], q_rs.at[0], dict(to_n, lon=lon_e)), has_n & has_e, has_s & has_w),
        (copy(col_ed.at[:, 7, :], cor.at[1, 0], q_ss.at[1], q_rs.at[1], dict(to_n, lon=lon_w)), has_n & has_w, has_s & has_e),
        (copy(col_ed.at[:, 0, :], cor.at[0, 1], q_ss.at[2], q_rs.at[2], dict(to_s, lon=lon_e)), has_s & has_e, has_n & has_w),
        (copy(col_ed.at[:, 0, :], cor.at[0, 0], q_ss.at[3], q_rs.at[3], dict(to_s, lon=lon_w)), has_s & has_w, has_n & has_e),
    ]
    flow_out = [
        copy(o_send.at[0:2, pl.ds(p * share, share)], out.at[0:2, :, :, cols(col)], uv_ss.at[d], uv_rs.at[d], {"lon": p})
        for d, p in others(1)
    ]
    warm_out = [
        copy(o_send.at[2, pl.ds(p * share, share)], out.at[2, :, :, cols(col)], t_ss.at[d], t_rs.at[d], {"lon": p})
        for d, p in others(1)
    ]
    heat_out = [
        copy(o_send.at[3, pl.ds(p * share, share)], out.at[3, :, :, cols(col)], h_ss.at[d], h_rs.at[d], {"lon": p})
        for d, p in others(1)
    ]

    lane = lax.broadcasted_iota(jnp.int32, (ROWS, LANES), 1)
    row = lax.broadcasted_iota(jnp.int32, (ROWS, LANES), 0)
    eastern, western = lane % STEP == 0, lane % STEP == STEP - 1

    def spots(axis):
        return lax.broadcasted_iota(jnp.int32, (LANES, LANES), axis)

    def twice(mask):
        one = mask.astype(F32).astype(jnp.bfloat16)
        return jnp.concatenate([one, one], axis=0)

    far_lane = (spots(1) + STEP // 2) % STEP
    take = twice(spots(0) == (far_lane + LANES - STEP // 2) % LANES)
    give = twice(
        ((spots(0) % STEP == 0) & (spots(1) == LANES - 1)) | ((spots(0) % STEP == STEP - 1) & (spots(1) == 0))
    )

    def unpack(a, b):
        parts = halves(jnp.concatenate([a, b], axis=0))
        place = lax.broadcasted_iota(jnp.int32, (1, WIDE), 1) % LANES
        only = [
            ((place + 1) % LANES // STEP == t).astype(F32).astype(jnp.bfloat16) for t in range(tracers)
        ]
        e = jnp.dot(jnp.concatenate([parts * o for o in only], axis=0), give, preferred_element_type=F32)
        return [[e[(2 * t + i) * ROWS : (2 * t + i + 1) * ROWS] for i in range(2)] for t in range(tracers)]

    for load in strip_loads:
        load.wait()
    blank = jnp.zeros((ROWS, LANES), F32)
    for p in range(nlon):
        acc = blank
        for f in range(4):
            for l in range(share):
                g = GROUP * (f * share + l)
                e = stage[p + 1, slot(f, l)] if p < nlon - 1 else blank
                w = stage[p - 1, slot(f, l)] if p > 0 else blank
                both = jnp.where(lane < LANES // 2, e, w)
                acc = jnp.where((lane + (3 + LANES - g)) % LANES < 5, pltpu.roll(both, g, 1), acc)
        stage[p, 3 * share] = acc

    pl.semaphore_wait(barrier, nlon - 1 + nlon * (jnp.minimum(s, 1) + jnp.minimum(nstrip - 1 - s, 1)))
    start(has_n, rows_n[::-1] + depth_n)
    start(has_s, rows_s[::-1] + depth_s)
    start(None, x_main)
    start(has_n, near_n)
    start(has_s, near_s)

    loads[1].wait()
    for k in range(depth):
        picked = jnp.dot(
            jnp.concatenate([halves(c_in[t, k]) for t in range(tracers)], axis=0), take, preferred_element_type=F32
        )
        acc = picked[0:ROWS]
        for t in range(1, tracers):
            here = (lane >= STEP * t - 2) & (lane < STEP * t + 2)
            acc = jnp.where(here, picked[t * ROWS : (t + 1) * ROWS], acc)
        col_ed[k] = acc
        if k % PAIR == 0:
            even = acc
        else:
            moved = pltpu.roll(acc, STEP // 2, 1)
            send_w[k // PAIR] = jnp.where(lane % STEP < 2, even, moved)
            send_e[k // PAIR] = jnp.where(lane % STEP < 2, moved, even)
    start(has_e, edge_e)
    start(has_w, edge_w)
    for c, send, _ in corners:
        start(send, [c])
    start(has_n, far_n)
    start(has_s, far_s)

    @pl.when(jnp.logical_not(has_s))
    def _():
        tall[:, :, 13:16, :] = jnp.zeros((nlon, 4 * share + 1, 3, LANES), F32)
        cnt[14:16, :] = jnp.zeros((2, nlon * LANES), jnp.int32)
        row_s[...] = jnp.zeros_like(row_s)

    @pl.when(jnp.logical_not(has_n))
    def _():
        tall[:, :, 8:10, :] = jnp.zeros((nlon, 4 * share + 1, 2, LANES), F32)
        cnt[8:10, :] = jnp.zeros((2, nlon * LANES), jnp.int32)
        row_n[...] = jnp.zeros_like(row_n)

    @pl.when(jnp.logical_not(has_w))
    def _():
        got_w[...] = jnp.zeros_like(got_w)

    @pl.when(jnp.logical_not(has_e))
    def _():
        got_e[...] = jnp.zeros_like(got_e)

    for i, there in enumerate((has_n, has_s)):
        for j, beside in enumerate((has_e, has_w)):

            @pl.when(jnp.logical_not(there & beside))
            def _(i=i, j=j):
                cor[i, j] = jnp.zeros((depth, LANES), F32)

    loads[0].wait()
    loads[2].wait()
    tall[col, :, 0:ROWS] = stage[col]
    lead_rates = [jnp.broadcast_to(r_in[0:1, b : b + 1], (ROWS, LANES)) for b in range(tracers)]

    high = tracers * ROWS
    spread = (
        lax.broadcasted_iota(jnp.int32, (high, tracers), 0) // ROWS
        == lax.broadcasted_iota(jnp.int32, (high, tracers), 1)
    ).astype(F32)
    gather = (
        lax.broadcasted_iota(jnp.int32, (tracers, high), 1) // ROWS
        == lax.broadcasted_iota(jnp.int32, (tracers, high), 0)
    ).astype(F32)
    rates = jnp.dot(
        spread, jnp.dot(r_in[...], gather, precision=EXACT, preferred_element_type=F32),
        precision=EXACT, preferred_element_type=F32,
    )
    same_row = (
        lax.broadcasted_iota(jnp.int32, (high, high), 0) % ROWS
        == lax.broadcasted_iota(jnp.int32, (high, high), 1) % ROWS
    )
    rates = split(jnp.where(same_row, rates, 0.0))
    spot0 = lax.broadcasted_iota(jnp.int32, (LANES, tracers), 0)
    pick0 = ((spot0 + 1) % LANES // STEP == lax.broadcasted_iota(jnp.int32, (LANES, tracers), 1)).astype(F32)
    spot1 = lax.broadcasted_iota(jnp.int32, (tracers, LANES), 1)
    pick1 = ((spot1 + 1) % LANES // STEP == lax.broadcasted_iota(jnp.int32, (tracers, LANES), 0)).astype(F32)
    across = jnp.dot(
        lax.dot_general(
            pick0, r_in[...], (((1,), (1,)), ((), ())), precision=EXACT, preferred_element_type=F32
        ),
        pick1, precision=EXACT, preferred_element_type=F32,
    )
    side_a = lax.broadcasted_iota(jnp.int32, (LANES, LANES), 0) % STEP
    side_b = lax.broadcasted_iota(jnp.int32, (LANES, LANES), 1) % STEP
    across = split(jnp.where((side_a == side_b) & ((side_a == 0) | (side_a == STEP - 1)), across, 0.0))

    wait_recv(has_s, rows_n[:1] + depth_n)
    wait_recv(has_n, rows_s[:1] + depth_s)

    lane2 = lax.broadcasted_iota(jnp.int32, (EXT, LANES), 1)
    window = (lane2 < 2) | (lane2 >= LANES - 3)

    def field(f, q, l):
        g = GROUP * (f * share + l)
        held = tall[q, 3 * share]
        moved = pltpu.roll(held, (LANES - g) % LANES, 1) if g else held
        return jnp.concatenate([tall[q, slot(f, l)], jnp.where(window, moved, 0.0)], axis=1)

    wet_e = jnp.where((lane2 < 2) & has_e, cnt[:, cols(lon_e)], 0)
    wet_w = jnp.where((lane2 >= LANES - 3) & has_w, cnt[:, cols(lon_w)], 0)
    n_main = cnt[:, cols(col)]
    n_side = jnp.where(lane2 < LANES // 2, wet_e, wet_w)
    layers = jnp.concatenate([n_main, n_side], axis=1)
    level_main = n_main[0:ROWS]

    line = lax.broadcasted_iota(jnp.int32, (EXT, WIDE), 0)
    spot = (s * ROWS + jnp.where(line < 12, line, line - EXT)).astype(F32)
    fcor = 0.3 * (2.0 * (spot + 0.5) / (nstrip * ROWS) - 1.0)

    layers_u, layers_v = jnp.minimum(layers, east(layers)), jnp.minimum(layers, north(layers))

    def masks(k):
        return [(k < n).astype(F32) for n in (layers, layers_u, layers_v)]

    def advance(m, u, v, t):
        push = 0.2 * t
        new_u = m[1] * (0.6 * u + east(0.1 * u - push) + 0.1 * (west(u) + north(u) + south(u)) + fcor * v + push)
        new_v = m[2] * (0.6 * v + north(0.1 * v - push) + 0.1 * (east(v) + west(v) + south(v)) - fcor * u + push)
        return new_u, new_v

    def both_steps(q):
        for l in range(share):
            k = q * share + l
            m = masks(k)
            u0, v0, t0, h0 = (field(f, q, l) for f in range(4))
            u1, v1 = advance(m, u0, v0, t0)
            for i, a in enumerate(upwind(u1, west(u1), v1, south(v1))):
                cex[i, k] = a[:, 0:LANES]
                cec[i, k] = a[0:ROWS, LANES:WIDE]
            t1 = m[0] * (t0 + 0.1 * lap(t0) + 0.5 * h0)
            u2, v2 = advance(m, u1, v1, t1)
            u_here, v_here = u2[0:ROWS, 0:LANES], v2[0:ROWS, 0:LANES]
            u_back, v_back = west(u2)[0:ROWS, 0:LANES], south(v2)[0:ROWS, 0:LANES]
            for i, a in enumerate(upwind(u_here, u_back, v_here, v_back)):
                cf1[i, k] = a
            t_base[k] = (m[0] * (t1 + 0.1 * lap(t1)))[0:ROWS, 0:LANES]
            o_send[0, k] = u_here
            o_send[1, k] = v_here

    both_steps(col)
    for d, _ in others(1):
        wait_recv(has_s, rows_n[d : d + 1])
        wait_recv(has_n, rows_s[d : d + 1])
        wait_recv(None, x_main[d - 1 : d])
        both_steps(lax.rem(col + nlon - d, nlon))
    out[0:2, :, :, cols(col)] = o_send[0:2, mine]

    def coefs(m, k):
        if m == 0:
            return [cex[i, k, 0:ROWS, :] for i in range(5)]
        return [cf1[i, k] for i in range(5)]

    def advect(a, x, edge, above, below):
        x_n = jnp.where(row == ROWS - 1, above, pltpu.roll(x, ROWS - 1, 0))
        x_s = jnp.where(row == 0, below, pltpu.roll(x, 1, 0))
        x_e = jnp.where(lane == LANES - 1, edge, pltpu.roll(x, LANES - 1, 1))
        x_w = jnp.where(lane == 0, edge, pltpu.roll(x, 1, 1))
        return mix(a, x, x_e, x_w, x_n, x_s)

    def lead_of(values):
        parts = [v * a for v, a in zip(values, lead_rates)]
        while len(parts) > 1:
            parts = [sum(parts[i : i + 2]) for i in range(0, len(parts), 2)]
        return parts[0]

    def shine(m, leads):
        tau, top = jnp.zeros((ROWS, LANES), F32), jnp.ones((ROWS, LANES), F32)
        tops = []
        for k, lead in enumerate(leads):
            wet_k = (k < level_main).astype(F32)
            tau = tau + (0.1 + 0.3 * jnp.maximum(lead, 0.0))
            under = jnp.exp(-tau)
            heat = 2.0 * wet_k * (top - under)
            if m == 0:
                o_send[2, k] = t_base[k] + 0.5 * wet_k * heat
            else:
                o_send[3, k] = heat
            tops.append(top)
            top = under
        start(None, heat_out if m else warm_out)
        out[2 + m, :, :, cols(col)] = o_send[2 + m, mine]
        return tops

    def react(blocks):
        parts = [split(a) for a in blocks]
        r = product(
            rates, (jnp.concatenate([a for a, _ in parts], axis=1), jnp.concatenate([b for _, b in parts], axis=1))
        )
        return [r[:, i * LANES : (i + 1) * LANES].reshape(tracers, ROWS, LANES) for i in range(len(blocks))]

    def settle(k, top, value, gain):
        return (k < level_main).astype(F32) * (value + (0.5 * top) * gain)

    def sideways(k):
        e, w = got_e[k // PAIR], got_w[k // PAIR]
        if k % PAIR:
            e, w = (pltpu.roll(x, LANES - STEP // 2, 1) for x in (e, w))
        return jnp.where(lane % STEP < 2, e, w)

    def ring_rows():
        tops, wets = [], []
        ends = unpack(*(jnp.where(lane % STEP < 2, cor[i, 0], cor[i, 1]) for i in range(2)))
        for i in range(2):
            rows, line_at, inner = (row_n, 8, 7) if i == 0 else (row_s, 15, 0)
            a = [cex[j, :, line_at, :] for j in range(5)]
            values = []
            for t in range(tracers):
                x, far, near = rows[0, t], rows[1, t], c_in[t, :, inner, :]
                edge = ends[t][i]
                x_e = jnp.where(lane == LANES - 1, edge, pltpu.roll(x, LANES - 1, 1))
                x_w = jnp.where(lane == 0, edge, pltpu.roll(x, 1, 1))
                x_n, x_s = (far, near) if i == 0 else (near, far)
                values.append(mix(a, x, x_e, x_w, x_n, x_s))
                (raw_n, raw_s)[i][t] = values[t]
            tau = 0.1 + 0.3 * jnp.maximum(values[0], 0.0)
            tau = jnp.where(row > 0, pltpu.roll(tau, 1, 0), 0.0)
            for shift in (1, 2, 4):
                tau = tau + jnp.where(row >= shift, pltpu.roll(tau, shift, 0), 0.0)
            top = jnp.exp(-tau)
            wet = (row < n_main[line_at : line_at + 1, :]).astype(F32)
            (lead_n, lead_s)[i][...] = wet * (values[0] + (0.5 * top) * lead_of(values))
            tops.append(top)
            wets.append(wet)
        return tops, wets

    def ring_finish(tops, wets):
        blocks = [a[...] for a in (raw_n, raw_s)]
        gains = react([a.reshape(high, LANES) for a in blocks])
        for i, ring in enumerate((ring_n, ring_s)):
            ring[...] = wets[i] * (blocks[i] + (0.5 * tops[i]) * gains[i])

    def ring_cols():
        def both(x):
            return jnp.where(
                eastern, jnp.broadcast_to(x[:, 0:1], x.shape), jnp.broadcast_to(x[:, LANES - 1 :], x.shape)
            )

        edge_n = jnp.where(lane % STEP < 2, cor[0, 0], cor[0, 1])
        edge_s = jnp.where(lane % STEP < 2, cor[1, 0], cor[1, 1])
        wet_n = both(n_side[0:ROWS])
        tau = jnp.zeros((ROWS, LANES), F32)
        values, tops = [], []
        for k in range(depth):
            x, own = sideways(k), col_ed[k]
            a = [both(cec[i, k]) for i in range(5)]
            x_e = pltpu.roll(jnp.where(eastern, own, x), LANES - 1, 1)
            x_w = pltpu.roll(jnp.where(western, own, x), 1, 1)
            x_n = jnp.where(row == ROWS - 1, edge_n[k : k + 1, :], pltpu.roll(x, ROWS - 1, 0))
            x_s = jnp.where(row == 0, edge_s[k : k + 1, :], pltpu.roll(x, 1, 0))
            value = mix(a, x, x_e, x_w, x_n, x_s)
            values.append(value)
            tops.append(jnp.exp(-tau))
            tau = tau + (0.1 + 0.3 * jnp.maximum(both(value), 0.0))
        r = product(split(jnp.concatenate(values, axis=0)), across)
        for k in range(depth):
            wet = (k < wet_n).astype(F32)
            ring_c[k] = wet * (values[k] + (0.5 * tops[k]) * r[k * ROWS : (k + 1) * ROWS])

    groups = [range(g, g + PAIR) for g in range(0, depth, PAIR)]
    wait_recv(has_s, near_n)
    wait_recv(has_n, near_s)
    wait_recv(has_w, edge_e)
    wait_recv(has_e, edge_w)
    start(None, flow_out)
    leads, firsts = [], []
    for levels in groups:
        edges = unpack(*(sideways(k) for k in levels))
        for i, k in enumerate(levels):
            a = coefs(0, k)
            values = [
                advect(a, c_in[t, k], edges[t][i], row_n[0, t, k : k + 1, :], row_s[0, t, k : k + 1, :])
                for t in range(tracers)
            ]
            for t in range(tracers):
                c_raw[t, k] = values[t]
            leads.append(values[0])
            firsts.append(lead_of(values))
    tops = shine(0, leads)
    for k in range(depth):
        lead_c[k] = settle(k, tops[k], leads[k], firsts[k])

    wait_recv(has_s, far_n)
    wait_recv(has_n, far_s)
    for c, _, recv in corners:
        wait_recv(recv, [c])
    ring_cols()
    ring_light = ring_rows()
    leads = []
    for k in range(depth):
        x, beside = lead_c[k], ring_c[k]
        x_n = jnp.where(row == ROWS - 1, lead_n[k : k + 1, :], pltpu.roll(x, ROWS - 1, 0))
        x_s = jnp.where(row == 0, lead_s[k : k + 1, :], pltpu.roll(x, 1, 0))
        x_e = pltpu.roll(jnp.where(lane == 0, beside, x), LANES - 1, 1)
        x_w = pltpu.roll(jnp.where(lane == LANES - 1, beside, x), 1, 1)
        leads.append(mix(coefs(1, k), x, x_e, x_w, x_n, x_s))
    last = shine(1, leads)

    ring_finish(*ring_light)
    for levels in groups:
        blocks = [c_raw[:, k] for k in levels]
        gains = react([b.reshape(high, LANES) for b in blocks])
        for k, block, gain in zip(levels, blocks, gains):
            c_mid[:, k] = settle(k, tops[k], block, gain)
    for levels in groups:
        edges = unpack(*(ring_c[k] for k in levels))
        blocks = []
        for i, k in enumerate(levels):
            a = coefs(1, k)
            blocks.append(jnp.concatenate([leads[k]] + [
                advect(a, c_mid[t, k], edges[t][i], ring_n[t, k : k + 1, :], ring_s[t, k : k + 1, :])
                for t in range(1, tracers)
            ], axis=0))
        gains = react(blocks)
        for k, block, gain in zip(levels, blocks, gains):
            c_out[:, k] = settle(k, last[k], block.reshape(tracers, ROWS, LANES), gain)

    wait_send(None, x_main)
    wait_send(has_n, rows_n + depth_n + near_n + far_n)
    wait_send(has_s, rows_s + depth_s + near_s + far_s)
    wait_send(has_e, edge_e)
    wait_send(has_w, edge_w)
    for c, send, _ in corners:
        wait_send(send, [c])
    wait_send(None, flow_out + warm_out)
    wait_recv(None, flow_out + warm_out)
    wait_send(None, heat_out)
    wait_recv(None, heat_out)


def store(out, c_out, u_dst, v_dst, t_dst, h_dst, c_dst, sem):
    saves = [pltpu.make_async_copy(c_out, c_dst, sem.at[4])]
    saves += [pltpu.make_async_copy(out.at[i], b, sem.at[i]) for i, b in enumerate((u_dst, v_dst, t_dst, h_dst))]
    for save in saves:
        save.start()
    for save in saves:
        save.wait()


def shards(sizes, u, v, t, h, c, n, r):
    tracers, depth, share, nlon, _, _ = sizes
    width = nlon * LANES
    strip = jax.ShapeDtypeStruct(u.shape, F32)
    tile = (ROWS, LANES)
    dma = pltpu.SemaphoreType.DMA
    hbm = pl.BlockSpec(memory_space=pltpu.HBM)
    vmem = pl.BlockSpec(memory_space=pltpu.VMEM)
    buf = pltpu.VMEM
    line = (tracers, depth, LANES)
    pair = [dma((nlon,)), dma((nlon,))]
    held = pl.pallas_call(
        functools.partial(kernel, sizes),
        out_shape=(buf((4, share, ROWS, width), F32), buf(c.shape, F32)),
        in_specs=[hbm] * 7,
        out_specs=(vmem, vmem),
        scratch_shapes=[
            buf((nlon, 4 * share + 1) + tile, F32),
            buf((nlon, 4 * share + 1, EXT, LANES), F32),
            buf((2, depth, EXT, WIDE), F32),
            buf((EXT, width), jnp.int32),
            buf(c.shape, F32), buf(c.shape, F32), buf(c.shape, F32),
            buf((2,) + line, F32), buf((2,) + line, F32),
            buf(line, F32), buf(line, F32), buf(line, F32), buf(line, F32),
            buf((depth,) + tile, F32), *([buf((depth // PAIR,) + tile, F32)] * 4),
            buf((2, 2, depth, LANES), F32),
            buf((depth,) + tile, F32), buf((depth,) + tile, F32), buf((depth, LANES), F32), buf((depth, LANES), F32),
            buf((5, depth, EXT, LANES), F32),
            buf((5, depth) + tile, F32),
            buf((5, depth) + tile, F32),
            buf((depth,) + tile, F32),
            buf((4, depth) + tile, F32),
            buf(r.shape, F32),
            dma((3,)), dma((4, nlon)),
            *(pair * 3),
            dma((2,)), dma((2,)), dma((6,)), dma((6,)), dma((4,)), dma((4,)),
            *(pair * 3),
        ],
        compiler_params=pltpu.CompilerParams(
            collective_id=0, has_side_effects=True, vmem_limit_bytes=VMEM
        ),
    )(*(pltpu.with_memory_space_constraint(x, pltpu.HBM) for x in (u, v, t, h, c, n, r)))
    return pl.pallas_call(
        store,
        out_shape=(strip, strip, strip, strip, jax.ShapeDtypeStruct(c.shape, F32)),
        in_specs=[vmem] * 2,
        out_specs=(hbm,) * 5,
        scratch_shapes=[dma((5,))],
        compiler_params=pltpu.CompilerParams(vmem_limit_bytes=VMEM),
    )(*held)


def solution(mesh):
    nlon, nrole = mesh.shape["lon"], mesh.shape["role"]
    nstrip = mesh.shape["lat"] * nrole
    strip = P("lon", ("grp", "lat", "role"), None)
    tile = P(None, None, ("grp", "lat", "role"), "lon")

    def run(u, v, t, h, c, n, r):
        sizes = (c.shape[0], c.shape[1], u.shape[0] // nlon, nlon, nrole, nstrip)
        return jax.shard_map(
            functools.partial(shards, sizes),
            mesh=mesh,
            in_specs=(strip, strip, strip, strip, tile, P(("grp", "lat", "role"), None), P()),
            out_specs=(strip, strip, strip, strip, tile),
            check_vma=False,
        )(u, v, t, h, c, n, r)

    return run
```

```python
import functools

import jax
import jax.numpy as jnp
from jax import lax
from jax.experimental import pallas as pl
from jax.experimental.pallas import tpu as pltpu
from jax.sharding import PartitionSpec as P

ROWS = 8
LANES = 128
EXT = 2 * ROWS
WIDE = 2 * LANES
PAIR = 2
STEP = 4
GROUP = 8
VMEM = 40 * 1024 * 1024
F32 = jnp.float32
EXACT = lax.Precision.HIGHEST


def east(q):
    return pltpu.roll(q, q.shape[-1] - 1, q.ndim - 1)


def west(q):
    return pltpu.roll(q, 1, q.ndim - 1)


def north(q):
    return pltpu.roll(q, q.shape[-2] - 1, q.ndim - 2)


def south(q):
    return pltpu.roll(q, 1, q.ndim - 2)


def lap(q):
    return east(q) + west(q) + north(q) + south(q) - 4.0 * q


def upwind(u, u_w, v, v_s):
    u_neg, v_neg = jnp.minimum(u, 0.0), jnp.minimum(v, 0.0)
    uw_pos, vs_pos = jnp.maximum(u_w, 0.0), jnp.maximum(v_s, 0.0)
    a_0 = 1.0 - 0.5 * (
        (jnp.maximum(u, 0.0) - jnp.minimum(u_w, 0.0)) + (jnp.maximum(v, 0.0) - jnp.minimum(v_s, 0.0))
    )
    return a_0, -0.5 * u_neg, 0.5 * uw_pos, -0.5 * v_neg, 0.5 * vs_pos


def mix(a, x, x_e, x_w, x_n, x_s):
    return a[0] * x + (a[1] * x_e + a[2] * x_w) + (a[3] * x_n + a[4] * x_s)


def split(a):
    hi = a.astype(jnp.bfloat16)
    return hi, (a - hi.astype(F32)).astype(jnp.bfloat16)


def halves(a):
    return jnp.concatenate(split(a), axis=1)


def product(a, b):
    a_hi, a_lo = a
    b_hi, b_lo = b
    return (
        jnp.dot(a_hi, b_hi, preferred_element_type=F32)
        + jnp.dot(a_hi, b_lo, preferred_element_type=F32)
        + jnp.dot(a_lo, b_hi, preferred_element_type=F32)
    )


def kernel(
    sizes,
    u_hbm, v_hbm, t_hbm, h_hbm, c_hbm, n_hbm, r_hbm,
    out, c_out,
    stage, tall, flow, cnt, c_in, c_east, c_west, c_raw, c_mid, row_n, row_s, raw_n, raw_s, ring_n, ring_s,
    col_ed, send_e, send_w, got_e, got_w, cor, ring_c, lead_c, lead_n, lead_s, cex, cec, cf1, t_base, o_send, r_in, in_sem, strip_sem,
    x_ss, x_rs, n_ss, n_rs, s_ss, s_rs,
    k_ss, k_rs, c_ss, c_rs, q_ss, q_rs, uv_ss, uv_rs, t_ss, t_rs, h_ss, h_rs,
):
    tracers, depth, share, nlon, nrole, nstrip = sizes
    def slot(f, l):
        return (0, 2 * share, share, 3 * share + 1)[f] + l

    strip_loads = [
        pltpu.make_async_copy(
            a.at[:, :, p * LANES : (p + 1) * LANES], stage.at[p, slot(f, 0) : slot(f, 0) + share], strip_sem.at[f, p]
        )
        for f, a in enumerate((u_hbm, v_hbm, t_hbm, h_hbm))
        for p in range(nlon)
    ]
    loads = [
        pltpu.make_async_copy(a, b, in_sem.at[i])
        for i, (a, b) in enumerate(((n_hbm, cnt.at[0:ROWS]), (c_hbm, c_in), (r_hbm, r_in)))
    ]
    for load in strip_loads + loads:
        load.start()

    s = lax.axis_index("lat") * nrole + lax.axis_index("role")
    col = lax.axis_index("lon")
    has_n, has_s = s < nstrip - 1, s > 0
    has_e, has_w = col < nlon - 1, col > 0
    sn, ss = lax.rem(s + 1, nstrip), lax.rem(s + nstrip - 1, nstrip)
    to_n = {"lat": sn // nrole, "role": lax.rem(sn, nrole)}
    to_s = {"lat": ss // nrole, "role": lax.rem(ss, nrole)}
    lon_e, lon_w = lax.rem(col + 1, nlon), lax.rem(col + nlon - 1, nlon)

    def others(first):
        return [(d, lax.rem(col + d, nlon)) for d in range(first, nlon)]

    barrier = pltpu.get_barrier_semaphore()

    def greet(dev):
        pl.semaphore_signal(barrier, inc=1, device_id=dev, device_id_type=pl.DeviceIdType.MESH)

    for d, p in others(1):
        greet({"lon": p})

    @pl.when(has_n)
    def _():
        for d, p in others(0):
            greet(dict(to_n, lon=p))

    @pl.when(has_s)
    def _():
        for d, p in others(0):
            greet(dict(to_s, lon=p))

    def copy(src, dst, ssem, rsem, dev):
        return pltpu.make_async_remote_copy(
            src_ref=src, dst_ref=dst, send_sem=ssem, recv_sem=rsem,
            device_id=dev, device_id_type=pl.DeviceIdType.MESH,
        )

    def start(cond, copies):
        if cond is None:
            for c in copies:
                c.start()
        else:
            pl.when(cond)(lambda: start(None, copies))

    def wait_recv(cond, copies):
        if cond is None:
            for c in copies:
                c.wait_recv()
        else:
            pl.when(cond)(lambda: wait_recv(None, copies))

    def wait_send(cond, copies):
        if cond is None:
            for c in copies:
                c.wait_send()
        else:
            pl.when(cond)(lambda: wait_send(None, copies))

    def cols(p):
        return pl.ds(pl.multiple_of(p * LANES, LANES), LANES)

    mine = pl.ds(col * share, share)
    x_main = [
        copy(stage.at[p], tall.at[col, :, 0:ROWS], x_ss.at[d], x_rs.at[d], {"lon": p})
        for d, p in others(1)
    ]
    late, last = 3 * share + 1, 4 * share + 1
    cuts_n = ((0, 2 * share, 6, 8), (2 * share, late, 5, 8), (late, last, 7, 8))
    cuts_s = ((0, late, 0, 2), (late, last, 0, 1))

    def rows(cuts, ss, rs, dev, d, p):
        return [
            copy(
                stage.at[p, a:b, lo:hi], tall.at[col, a:b, ROWS + lo : ROWS + hi],
                ss.at[i, d], rs.at[i, d], dict(dev, lon=p),
            )
            for i, (a, b, lo, hi) in enumerate(cuts)
        ]

    rows_n = [rows(cuts_n if d else ((0, last, 5, 8),), n_ss, n_rs, to_n, d, p) for d, p in others(0)]
    rows_s = [rows(cuts_s if d else ((0, last, 0, 2),), s_ss, s_rs, to_s, d, p) for d, p in others(0)]
    depth_n = [copy(n_hbm.at[6:8], cnt.at[14:16], k_ss.at[0], k_rs.at[0], to_n)]
    depth_s = [copy(n_hbm.at[0:2], cnt.at[8:10], k_ss.at[1], k_rs.at[1], to_s)]
    near_n = [copy(c_hbm.at[:, :, 7, :], row_s.at[0], c_ss.at[0], c_rs.at[0], to_n)]
    near_s = [copy(c_hbm.at[:, :, 0, :], row_n.at[0], c_ss.at[1], c_rs.at[1], to_s)]
    far_n = [copy(c_hbm.at[:, :, 6, :], row_s.at[1], c_ss.at[2], c_rs.at[2], to_n)]
    far_s = [copy(c_hbm.at[:, :, 1, :], row_n.at[1], c_ss.at[3], c_rs.at[3], to_s)]
    edge_e = [copy(send_e, got_w, c_ss.at[4], c_rs.at[4], {"lon": lon_e})]
    edge_w = [copy(send_w, got_e, c_ss.at[5], c_rs.at[5], {"lon": lon_w})]
    corners = [
        (copy(col_ed.at[:, 7, :], cor.at[1, 1], q_ss.at[0], q_rs.at[0], dict(to_n, lon=lon_e)), has_n & has_e, has_s & has_w),
        (copy(col_ed.at[:, 7, :], cor.at[1, 0], q_ss.at[1], q_rs.at[1], dict(to_n, lon=lon_w)), has_n & has_w, has_s & has_e),
        (copy(col_ed.at[:, 0, :], cor.at[0, 1], q_ss.at[2], q_rs.at[2], dict(to_s, lon=lon_e)), has_s & has_e, has_n & has_w),
        (copy(col_ed.at[:, 0, :], cor.at[0, 0], q_ss.at[3], q_rs.at[3], dict(to_s, lon=lon_w)), has_s & has_w, has_n & has_e),
    ]
    flow_out = [
        copy(o_send.at[0:2, pl.ds(p * share, share)], out.at[0:2, :, :, cols(col)], uv_ss.at[d], uv_rs.at[d], {"lon": p})
        for d, p in others(1)
    ]
    warm_out = [
        copy(o_send.at[2, pl.ds(p * share, share)], out.at[2, :, :, cols(col)], t_ss.at[d], t_rs.at[d], {"lon": p})
        for d, p in others(1)
    ]
    heat_out = [
        copy(o_send.at[3, pl.ds(p * share, share)], out.at[3, :, :, cols(col)], h_ss.at[d], h_rs.at[d], {"lon": p})
        for d, p in others(1)
    ]

    lane = lax.broadcasted_iota(jnp.int32, (ROWS, LANES), 1)
    row = lax.broadcasted_iota(jnp.int32, (ROWS, LANES), 0)
    eastern, western = lane % STEP == 0, lane % STEP == STEP - 1

    def spots(axis):
        return lax.broadcasted_iota(jnp.int32, (LANES, LANES), axis)

    def twice(mask):
        one = mask.astype(F32).astype(jnp.bfloat16)
        return jnp.concatenate([one, one], axis=0)

    far_lane = (spots(1) + STEP // 2) % STEP
    take = twice(spots(0) == (far_lane + LANES - STEP // 2) % LANES)
    give = twice(
        ((spots(0) % STEP == 0) & (spots(1) == LANES - 1)) | ((spots(0) % STEP == STEP - 1) & (spots(1) == 0))
    )

    def unpack(a, b):
        parts = halves(jnp.concatenate([a, b], axis=0))
        place = lax.broadcasted_iota(jnp.int32, (1, WIDE), 1) % LANES
        only = [
            ((place + 1) % LANES // STEP == t).astype(F32).astype(jnp.bfloat16) for t in range(tracers)
        ]
        e = jnp.dot(jnp.concatenate([parts * o for o in only], axis=0), give, preferred_element_type=F32)
        return [[e[(2 * t + i) * ROWS : (2 * t + i + 1) * ROWS] for i in range(2)] for t in range(tracers)]

    for load in strip_loads:
        load.wait()
    blank = jnp.zeros((ROWS, LANES), F32)
    for p in range(nlon):
        acc = blank
        for f in range(4):
            for l in range(share):
                g = GROUP * (f * share + l)
                e = stage[p + 1, slot(f, l)] if p < nlon - 1 else blank
                w = stage[p - 1, slot(f, l)] if p > 0 else blank
                both = jnp.where(lane < LANES // 2, e, w)
                acc = jnp.where((lane + (3 + LANES - g)) % LANES < 5, pltpu.roll(both, g, 1), acc)
        stage[p, 3 * share] = acc

    pl.semaphore_wait(barrier, nlon - 1 + nlon * (jnp.minimum(s, 1) + jnp.minimum(nstrip - 1 - s, 1)))
    start(has_n, sum(rows_n[1:], []))
    start(has_s, sum(rows_s[1:], []))
    start(None, x_main)
    start(has_n, rows_n[0] + depth_n)
    start(has_s, rows_s[0] + depth_s)
    start(has_n, near_n)
    start(has_s, near_s)

    loads[1].wait()
    for k in range(depth):
        picked = jnp.dot(
            jnp.concatenate([halves(c_in[t, k]) for t in range(tracers)], axis=0), take, preferred_element_type=F32
        )
        acc = picked[0:ROWS]
        for t in range(1, tracers):
            here = (lane >= STEP * t - 2) & (lane < STEP * t + 2)
            acc = jnp.where(here, picked[t * ROWS : (t + 1) * ROWS], acc)
        col_ed[k] = acc
        if k % PAIR == 0:
            even = acc
        else:
            moved = pltpu.roll(acc, STEP // 2, 1)
            send_w[k // PAIR] = jnp.where(lane % STEP < 2, even, moved)
            send_e[k // PAIR] = jnp.where(lane % STEP < 2, moved, even)
    start(has_e, edge_e)
    start(has_w, edge_w)
    for c, send, _ in corners:
        start(send, [c])
    start(has_n, far_n)
    start(has_s, far_s)

    @pl.when(jnp.logical_not(has_s))
    def _():
        tall[:, :, 13:16, :] = jnp.zeros((nlon, 4 * share + 1, 3, LANES), F32)
        cnt[14:16, :] = jnp.zeros((2, nlon * LANES), jnp.int32)
        row_s[...] = jnp.zeros_like(row_s)

    @pl.when(jnp.logical_not(has_n))
    def _():
        tall[:, :, 8:10, :] = jnp.zeros((nlon, 4 * share + 1, 2, LANES), F32)
        cnt[8:10, :] = jnp.zeros((2, nlon * LANES), jnp.int32)
        row_n[...] = jnp.zeros_like(row_n)

    @pl.when(jnp.logical_not(has_w))
    def _():
        got_w[...] = jnp.zeros_like(got_w)

    @pl.when(jnp.logical_not(has_e))
    def _():
        got_e[...] = jnp.zeros_like(got_e)

    for i, there in enumerate((has_n, has_s)):
        for j, beside in enumerate((has_e, has_w)):

            @pl.when(jnp.logical_not(there & beside))
            def _(i=i, j=j):
                cor[i, j] = jnp.zeros((depth, LANES), F32)

    loads[0].wait()
    loads[2].wait()
    tall[col, :, 0:ROWS] = stage[col]
    lead_rates = [jnp.broadcast_to(r_in[0:1, b : b + 1], (ROWS, LANES)) for b in range(tracers)]

    high = tracers * ROWS
    spread = (
        lax.broadcasted_iota(jnp.int32, (high, tracers), 0) // ROWS
        == lax.broadcasted_iota(jnp.int32, (high, tracers), 1)
    ).astype(F32)
    gather = (
        lax.broadcasted_iota(jnp.int32, (tracers, high), 1) // ROWS
        == lax.broadcasted_iota(jnp.int32, (tracers, high), 0)
    ).astype(F32)
    rates = jnp.dot(
        spread, jnp.dot(r_in[...], gather, precision=EXACT, preferred_element_type=F32),
        precision=EXACT, preferred_element_type=F32,
    )
    same_row = (
        lax.broadcasted_iota(jnp.int32, (high, high), 0) % ROWS
        == lax.broadcasted_iota(jnp.int32, (high, high), 1) % ROWS
    )
    rates = split(jnp.where(same_row, rates, 0.0))
    spot0 = lax.broadcasted_iota(jnp.int32, (LANES, tracers), 0)
    pick0 = ((spot0 + 1) % LANES // STEP == lax.broadcasted_iota(jnp.int32, (LANES, tracers), 1)).astype(F32)
    spot1 = lax.broadcasted_iota(jnp.int32, (tracers, LANES), 1)
    pick1 = ((spot1 + 1) % LANES // STEP == lax.broadcasted_iota(jnp.int32, (tracers, LANES), 0)).astype(F32)
    across = jnp.dot(
        lax.dot_general(
            pick0, r_in[...], (((1,), (1,)), ((), ())), precision=EXACT, preferred_element_type=F32
        ),
        pick1, precision=EXACT, preferred_element_type=F32,
    )
    side_a = lax.broadcasted_iota(jnp.int32, (LANES, LANES), 0) % STEP
    side_b = lax.broadcasted_iota(jnp.int32, (LANES, LANES), 1) % STEP
    across = split(jnp.where((side_a == side_b) & ((side_a == 0) | (side_a == STEP - 1)), across, 0.0))

    for k in range(depth):
        for t in range(tracers):
            c_east[t, k] = pltpu.roll(c_in[t, k], LANES - 1, 1)
            c_west[t, k] = pltpu.roll(c_in[t, k], 1, 1)

    wait_recv(has_s, rows_n[0] + depth_n)
    wait_recv(has_n, rows_s[0] + depth_s)

    lane2 = lax.broadcasted_iota(jnp.int32, (EXT, LANES), 1)
    window = (lane2 < 2) | (lane2 >= LANES - 3)

    def field(f, q, l):
        g = GROUP * (f * share + l)
        held = tall[q, 3 * share]
        moved = pltpu.roll(held, (LANES - g) % LANES, 1) if g else held
        return jnp.concatenate([tall[q, slot(f, l)], jnp.where(window, moved, 0.0)], axis=1)

    wet_e = jnp.where((lane2 < 2) & has_e, cnt[:, cols(lon_e)], 0)
    wet_w = jnp.where((lane2 >= LANES - 3) & has_w, cnt[:, cols(lon_w)], 0)
    n_main = cnt[:, cols(col)]
    n_side = jnp.where(lane2 < LANES // 2, wet_e, wet_w)
    layers = jnp.concatenate([n_main, n_side], axis=1)
    level_main = n_main[0:ROWS]

    line = lax.broadcasted_iota(jnp.int32, (EXT, WIDE), 0)
    spot = (s * ROWS + jnp.where(line < 12, line, line - EXT)).astype(F32)
    fcor = 0.3 * (2.0 * (spot + 0.5) / (nstrip * ROWS) - 1.0)

    layers_u, layers_v = jnp.minimum(layers, east(layers)), jnp.minimum(layers, north(layers))

    def masks(k):
        return [(k < n).astype(F32) for n in (layers, layers_u, layers_v)]

    def advance(m, u, v, t):
        push = 0.2 * t
        new_u = m[1] * (0.6 * u + east(0.1 * u - push) + 0.1 * (west(u) + north(u) + south(u)) + fcor * v + push)
        new_v = m[2] * (0.6 * v + north(0.1 * v - push) + 0.1 * (east(v) + west(v) + south(v)) - fcor * u + push)
        return new_u, new_v

    def both(x):
        return jnp.where(eastern, jnp.broadcast_to(x[:, 0:1], x.shape), jnp.broadcast_to(x[:, LANES - 1 :], x.shape))

    def both_steps(q):
        for l in range(share):
            k = q * share + l
            m = masks(k)
            u0, v0, t0, h0 = (field(f, q, l) for f in range(4))
            u1, v1 = advance(m, u0, v0, t0)
            for i, a in enumerate(upwind(u1, west(u1), v1, south(v1))):
                cex[i, k] = a[:, 0:LANES]
                cec[i, k] = both(a[0:ROWS, LANES:WIDE])
            t1 = m[0] * (t0 + 0.1 * lap(t0) + 0.5 * h0)
            u2, v2 = advance(m, u1, v1, t1)
            u_here, v_here = u2[0:ROWS, 0:LANES], v2[0:ROWS, 0:LANES]
            u_back, v_back = west(u2)[0:ROWS, 0:LANES], south(v2)[0:ROWS, 0:LANES]
            for i, a in enumerate(upwind(u_here, u_back, v_here, v_back)):
                cf1[i, k] = a
            t_base[k] = (m[0] * (t1 + 0.1 * lap(t1)))[0:ROWS, 0:LANES]
            o_send[0, k] = u_here
            o_send[1, k] = v_here

    both_steps(col)
    for d, _ in others(1):
        wait_recv(has_s, rows_n[d])
        wait_recv(has_n, rows_s[d])
        wait_recv(None, x_main[d - 1 : d])
        both_steps(lax.rem(col + nlon - d, nlon))
    out[0:2, :, :, cols(col)] = o_send[0:2, mine]

    def coefs(m, k):
        if m == 0:
            return [cex[i, k, 0:ROWS, :] for i in range(5)]
        return [cf1[i, k] for i in range(5)]

    def advect(a, x, edge, above, below, x_e=None, x_w=None):
        if x_e is None:
            x_e, x_w = pltpu.roll(x, LANES - 1, 1), pltpu.roll(x, 1, 1)
        x_n = jnp.where(row == ROWS - 1, above, pltpu.roll(x, ROWS - 1, 0))
        x_s = jnp.where(row == 0, below, pltpu.roll(x, 1, 0))
        x_e = jnp.where(lane == LANES - 1, edge, x_e)
        x_w = jnp.where(lane == 0, edge, x_w)
        return mix(a, x, x_e, x_w, x_n, x_s)

    def lead_of(values):
        parts = [v * a for v, a in zip(values, lead_rates)]
        while len(parts) > 1:
            parts = [sum(parts[i : i + 2]) for i in range(0, len(parts), 2)]
        return parts[0]

    def shine(m, leads):
        tau, top = jnp.zeros((ROWS, LANES), F32), jnp.ones((ROWS, LANES), F32)
        tops = []
        for k, lead in enumerate(leads):
            wet_k = (k < level_main).astype(F32)
            tau = tau + (0.1 + 0.3 * jnp.maximum(lead, 0.0))
            under = jnp.exp(-tau)
            heat = 2.0 * wet_k * (top - under)
            if m == 0:
                o_send[2, k] = t_base[k] + 0.5 * wet_k * heat
            else:
                o_send[3, k] = heat
            tops.append(top)
            top = under
        start(None, heat_out if m else warm_out)
        out[2 + m, :, :, cols(col)] = o_send[2 + m, mine]
        return tops

    def react(blocks):
        parts = [split(a) for a in blocks]
        r = product(
            rates, (jnp.concatenate([a for a, _ in parts], axis=1), jnp.concatenate([b for _, b in parts], axis=1))
        )
        return [r[:, i * LANES : (i + 1) * LANES].reshape(tracers, ROWS, LANES) for i in range(len(blocks))]

    def settle(k, top, value, gain):
        return (k < level_main).astype(F32) * (value + (0.5 * top) * gain)

    def sideways(k):
        e, w = got_e[k // PAIR], got_w[k // PAIR]
        if k % PAIR:
            e, w = (pltpu.roll(x, LANES - STEP // 2, 1) for x in (e, w))
        return jnp.where(lane % STEP < 2, e, w)

    def ring_rows():
        tops, wets = [], []
        ends = unpack(*(jnp.where(lane % STEP < 2, cor[i, 0], cor[i, 1]) for i in range(2)))
        for i in range(2):
            rows, line_at, inner = (row_n, 8, 7) if i == 0 else (row_s, 15, 0)
            a = [cex[j, :, line_at, :] for j in range(5)]
            values = []
            for t in range(tracers):
                x, far, near = rows[0, t], rows[1, t], c_in[t, :, inner, :]
                edge = ends[t][i]
                x_e = jnp.where(lane == LANES - 1, edge, pltpu.roll(x, LANES - 1, 1))
                x_w = jnp.where(lane == 0, edge, pltpu.roll(x, 1, 1))
                x_n, x_s = (far, near) if i == 0 else (near, far)
                values.append(mix(a, x, x_e, x_w, x_n, x_s))
                (raw_n, raw_s)[i][t] = values[t]
            tau = 0.1 + 0.3 * jnp.maximum(values[0], 0.0)
            tau = jnp.where(row > 0, pltpu.roll(tau, 1, 0), 0.0)
            for shift in (1, 2, 4):
                tau = tau + jnp.where(row >= shift, pltpu.roll(tau, shift, 0), 0.0)
            top = jnp.exp(-tau)
            wet = (row < n_main[line_at : line_at + 1, :]).astype(F32)
            (lead_n, lead_s)[i][...] = wet * (values[0] + (0.5 * top) * lead_of(values))
            tops.append(top)
            wets.append(wet)
        return tops, wets

    def ring_finish(tops, wets):
        blocks = [a[...] for a in (raw_n, raw_s)]
        gains = react([a.reshape(high, LANES) for a in blocks])
        for i, ring in enumerate((ring_n, ring_s)):
            ring[...] = wets[i] * (blocks[i] + (0.5 * tops[i]) * gains[i])

    def ring_cols():
        edge_n = jnp.where(lane % STEP < 2, cor[0, 0], cor[0, 1])
        edge_s = jnp.where(lane % STEP < 2, cor[1, 0], cor[1, 1])
        wet_n = both(n_side[0:ROWS])
        tau = jnp.zeros((ROWS, LANES), F32)
        values, tops = [], []
        for k in range(depth):
            x, own = sideways(k), col_ed[k]
            a = [cec[i, k] for i in range(5)]
            x_e = pltpu.roll(jnp.where(eastern, own, x), LANES - 1, 1)
            x_w = pltpu.roll(jnp.where(western, own, x), 1, 1)
            x_n = jnp.where(row == ROWS - 1, edge_n[k : k + 1, :], pltpu.roll(x, ROWS - 1, 0))
            x_s = jnp.where(row == 0, edge_s[k : k + 1, :], pltpu.roll(x, 1, 0))
            value = mix(a, x, x_e, x_w, x_n, x_s)
            values.append(value)
            tops.append(jnp.exp(-tau))
            tau = tau + (0.1 + 0.3 * jnp.maximum(both(value), 0.0))
        r = product(split(jnp.concatenate(values, axis=0)), across)
        for k in range(depth):
            wet = (k < wet_n).astype(F32)
            ring_c[k] = wet * (values[k] + (0.5 * tops[k]) * r[k * ROWS : (k + 1) * ROWS])

    groups = [range(g, g + PAIR) for g in range(0, depth, PAIR)]
    wait_recv(has_s, near_n)
    wait_recv(has_n, near_s)
    wait_recv(has_w, edge_e)
    wait_recv(has_e, edge_w)
    start(None, flow_out)
    leads, firsts = [], []
    for levels in groups:
        edges = unpack(*(sideways(k) for k in levels))
        for i, k in enumerate(levels):
            a = coefs(0, k)
            values = [
                advect(
                    a, c_in[t, k], edges[t][i], row_n[0, t, k : k + 1, :], row_s[0, t, k : k + 1, :],
                    c_east[t, k], c_west[t, k],
                )
                for t in range(tracers)
            ]
            for t in range(tracers):
                c_raw[t, k] = values[t]
            leads.append(values[0])
            firsts.append(lead_of(values))
    tops = shine(0, leads)
    for k in range(depth):
        lead_c[k] = settle(k, tops[k], leads[k], firsts[k])

    wait_recv(has_s, far_n)
    wait_recv(has_n, far_s)
    for c, _, recv in corners:
        wait_recv(recv, [c])
    ring_cols()
    ring_light = ring_rows()
    leads = []
    for k in range(depth):
        x, beside = lead_c[k], ring_c[k]
        x_n = jnp.where(row == ROWS - 1, lead_n[k : k + 1, :], pltpu.roll(x, ROWS - 1, 0))
        x_s = jnp.where(row == 0, lead_s[k : k + 1, :], pltpu.roll(x, 1, 0))
        x_e = pltpu.roll(jnp.where(lane == 0, beside, x), LANES - 1, 1)
        x_w = pltpu.roll(jnp.where(lane == LANES - 1, beside, x), 1, 1)
        leads.append(mix(coefs(1, k), x, x_e, x_w, x_n, x_s))
    last = shine(1, leads)

    ring_finish(*ring_light)
    for levels in groups:
        blocks = [c_raw[:, k] for k in levels]
        gains = react([b.reshape(high, LANES) for b in blocks])
        for k, block, gain in zip(levels, blocks, gains):
            c_mid[:, k] = settle(k, tops[k], block, gain)
    for levels in groups:
        edges = unpack(*(ring_c[k] for k in levels))
        blocks = []
        for i, k in enumerate(levels):
            a = coefs(1, k)
            blocks.append(jnp.concatenate([leads[k]] + [
                advect(a, c_mid[t, k], edges[t][i], ring_n[t, k : k + 1, :], ring_s[t, k : k + 1, :])
                for t in range(1, tracers)
            ], axis=0))
        gains = react(blocks)
        for k, block, gain in zip(levels, blocks, gains):
            c_out[:, k] = settle(k, last[k], block.reshape(tracers, ROWS, LANES), gain)

    wait_send(None, x_main)
    wait_send(has_n, sum(rows_n, []) + depth_n + near_n + far_n)
    wait_send(has_s, sum(rows_s, []) + depth_s + near_s + far_s)
    wait_send(has_e, edge_e)
    wait_send(has_w, edge_w)
    for c, send, _ in corners:
        wait_send(send, [c])
    wait_send(None, flow_out + warm_out)
    wait_recv(None, flow_out + warm_out)
    wait_send(None, heat_out)
    wait_recv(None, heat_out)


def store(out, c_out, u_dst, v_dst, t_dst, h_dst, c_dst, sem):
    saves = [pltpu.make_async_copy(c_out, c_dst, sem.at[4])]
    saves += [pltpu.make_async_copy(out.at[i], b, sem.at[i]) for i, b in enumerate((u_dst, v_dst, t_dst, h_dst))]
    for save in saves:
        save.start()
    for save in saves:
        save.wait()


def shards(sizes, u, v, t, h, c, n, r):
    tracers, depth, share, nlon, _, _ = sizes
    width = nlon * LANES
    strip = jax.ShapeDtypeStruct(u.shape, F32)
    tile = (ROWS, LANES)
    dma = pltpu.SemaphoreType.DMA
    hbm = pl.BlockSpec(memory_space=pltpu.HBM)
    vmem = pl.BlockSpec(memory_space=pltpu.VMEM)
    buf = pltpu.VMEM
    line = (tracers, depth, LANES)
    pair = [dma((nlon,)), dma((nlon,))]
    held = pl.pallas_call(
        functools.partial(kernel, sizes),
        out_shape=(buf((4, share, ROWS, width), F32), buf(c.shape, F32)),
        in_specs=[hbm] * 7,
        out_specs=(vmem, vmem),
        scratch_shapes=[
            buf((nlon, 4 * share + 1) + tile, F32),
            buf((nlon, 4 * share + 1, EXT, LANES), F32),
            buf((2, depth, EXT, WIDE), F32),
            buf((EXT, width), jnp.int32),
            *([buf(c.shape, F32)] * 5),
            buf((2,) + line, F32), buf((2,) + line, F32),
            buf(line, F32), buf(line, F32), buf(line, F32), buf(line, F32),
            buf((depth,) + tile, F32), *([buf((depth // PAIR,) + tile, F32)] * 4),
            buf((2, 2, depth, LANES), F32),
            buf((depth,) + tile, F32), buf((depth,) + tile, F32), buf((depth, LANES), F32), buf((depth, LANES), F32),
            buf((5, depth, EXT, LANES), F32),
            buf((5, depth) + tile, F32),
            buf((5, depth) + tile, F32),
            buf((depth,) + tile, F32),
            buf((4, depth) + tile, F32),
            buf(r.shape, F32),
            dma((3,)), dma((4, nlon)),
            *pair, dma((3, nlon)), dma((3, nlon)), dma((2, nlon)), dma((2, nlon)),
            dma((2,)), dma((2,)), dma((6,)), dma((6,)), dma((4,)), dma((4,)),
            *(pair * 3),
        ],
        compiler_params=pltpu.CompilerParams(
            collective_id=0, has_side_effects=True, vmem_limit_bytes=VMEM
        ),
    )(*(pltpu.with_memory_space_constraint(x, pltpu.HBM) for x in (u, v, t, h, c, n, r)))
    return pl.pallas_call(
        store,
        out_shape=(strip, strip, strip, strip, jax.ShapeDtypeStruct(c.shape, F32)),
        in_specs=[vmem] * 2,
        out_specs=(hbm,) * 5,
        scratch_shapes=[dma((5,))],
        compiler_params=pltpu.CompilerParams(vmem_limit_bytes=VMEM),
    )(*held)


def solution(mesh):
    nlon, nrole = mesh.shape["lon"], mesh.shape["role"]
    nstrip = mesh.shape["lat"] * nrole
    strip = P("lon", ("grp", "lat", "role"), None)
    tile = P(None, None, ("grp", "lat", "role"), "lon")

    def run(u, v, t, h, c, n, r):
        sizes = (c.shape[0], c.shape[1], u.shape[0] // nlon, nlon, nrole, nstrip)
        return jax.shard_map(
            functools.partial(shards, sizes),
            mesh=mesh,
            in_specs=(strip, strip, strip, strip, tile, P(("grp", "lat", "role"), None), P()),
            out_specs=(strip, strip, strip, strip, tile),
            check_vma=False,
        )(u, v, t, h, c, n, r)

    return run
```

```python
import functools

import jax
import jax.numpy as jnp
from jax import lax
from jax.experimental import pallas as pl
from jax.experimental.pallas import tpu as pltpu
from jax.sharding import PartitionSpec as P

ROWS = 8
LANES = 128
EXT = 2 * ROWS
WIDE = 2 * LANES
PAIR = 2
STEP = 4
GROUP = 8
VMEM = 40 * 1024 * 1024
F32 = jnp.float32
EXACT = lax.Precision.HIGHEST


def east(q):
    return pltpu.roll(q, q.shape[-1] - 1, q.ndim - 1)


def west(q):
    return pltpu.roll(q, 1, q.ndim - 1)


def north(q):
    return pltpu.roll(q, q.shape[-2] - 1, q.ndim - 2)


def south(q):
    return pltpu.roll(q, 1, q.ndim - 2)


def lap(q):
    return east(q) + west(q) + north(q) + south(q) - 4.0 * q


def upwind(u, u_w, v, v_s):
    u_neg, v_neg = jnp.minimum(u, 0.0), jnp.minimum(v, 0.0)
    uw_pos, vs_pos = jnp.maximum(u_w, 0.0), jnp.maximum(v_s, 0.0)
    a_0 = 1.0 - 0.5 * (
        (jnp.maximum(u, 0.0) - jnp.minimum(u_w, 0.0)) + (jnp.maximum(v, 0.0) - jnp.minimum(v_s, 0.0))
    )
    return a_0, -0.5 * u_neg, 0.5 * uw_pos, -0.5 * v_neg, 0.5 * vs_pos


def mix(a, x, x_e, x_w, x_n, x_s):
    return a[0] * x + (a[1] * x_e + a[2] * x_w) + (a[3] * x_n + a[4] * x_s)


def split(a):
    hi = a.astype(jnp.bfloat16)
    return hi, (a - hi.astype(F32)).astype(jnp.bfloat16)


def halves(a):
    return jnp.concatenate(split(a), axis=1)


def product(a, b):
    a_hi, a_lo = a
    b_hi, b_lo = b
    return (
        jnp.dot(a_hi, b_hi, preferred_element_type=F32)
        + jnp.dot(a_hi, b_lo, preferred_element_type=F32)
        + jnp.dot(a_lo, b_hi, preferred_element_type=F32)
    )


def kernel(
    sizes,
    u_hbm, v_hbm, t_hbm, h_hbm, c_hbm, n_hbm, r_hbm,
    out, c_out,
    stage, tall, flow, cnt, c_in, c_east, c_west, c_raw, c_mid, row_n, row_s, raw_n, raw_s, ring_n, ring_s,
    col_ed, send_e, send_w, got_e, got_w, cor, ring_c, lead_c, lead_n, lead_s, cex, cec, cf1, t_base, o_send, r_in, in_sem, strip_sem,
    x_ss, x_rs, n_ss, n_rs, s_ss, s_rs,
    k_ss, k_rs, c_ss, c_rs, q_ss, q_rs, uv_ss, uv_rs, t_ss, t_rs, h_ss, h_rs,
):
    tracers, depth, share, nlon, nrole, nstrip = sizes
    def slot(f, l):
        return (0, 2 * share, share, 3 * share + 1)[f] + l

    strip_loads = [
        pltpu.make_async_copy(
            a.at[:, :, p * LANES : (p + 1) * LANES], stage.at[p, slot(f, 0) : slot(f, 0) + share], strip_sem.at[f, p]
        )
        for f, a in enumerate((u_hbm, v_hbm, t_hbm, h_hbm))
        for p in range(nlon)
    ]
    loads = [
        pltpu.make_async_copy(a, b, in_sem.at[i])
        for i, (a, b) in enumerate(((n_hbm, cnt.at[0:ROWS]), (c_hbm, c_in), (r_hbm, r_in)))
    ]
    for load in strip_loads + loads:
        load.start()

    s = lax.axis_index("lat") * nrole + lax.axis_index("role")
    col = lax.axis_index("lon")
    has_n, has_s = s < nstrip - 1, s > 0
    has_e, has_w = col < nlon - 1, col > 0
    sn, ss = lax.rem(s + 1, nstrip), lax.rem(s + nstrip - 1, nstrip)
    to_n = {"lat": sn // nrole, "role": lax.rem(sn, nrole)}
    to_s = {"lat": ss // nrole, "role": lax.rem(ss, nrole)}
    lon_e, lon_w = lax.rem(col + 1, nlon), lax.rem(col + nlon - 1, nlon)

    def others(first):
        return [(d, lax.rem(col + d, nlon)) for d in range(first, nlon)]

    barrier = pltpu.get_barrier_semaphore()

    def greet(dev):
        pl.semaphore_signal(barrier, inc=1, device_id=dev, device_id_type=pl.DeviceIdType.MESH)

    for d, p in others(1):
        greet({"lon": p})

    @pl.when(has_n)
    def _():
        for d, p in others(0):
            greet(dict(to_n, lon=p))

    @pl.when(has_s)
    def _():
        for d, p in others(0):
            greet(dict(to_s, lon=p))

    def copy(src, dst, ssem, rsem, dev):
        return pltpu.make_async_remote_copy(
            src_ref=src, dst_ref=dst, send_sem=ssem, recv_sem=rsem,
            device_id=dev, device_id_type=pl.DeviceIdType.MESH,
        )

    def start(cond, copies):
        if cond is None:
            for c in copies:
                c.start()
        else:
            pl.when(cond)(lambda: start(None, copies))

    def wait_recv(cond, copies):
        if cond is None:
            for c in copies:
                c.wait_recv()
        else:
            pl.when(cond)(lambda: wait_recv(None, copies))

    def wait_send(cond, copies):
        if cond is None:
            for c in copies:
                c.wait_send()
        else:
            pl.when(cond)(lambda: wait_send(None, copies))

    def cols(p):
        return pl.ds(pl.multiple_of(p * LANES, LANES), LANES)

    mine = pl.ds(col * share, share)
    x_main = [
        copy(stage.at[p], tall.at[col, :, 0:ROWS], x_ss.at[d], x_rs.at[d], {"lon": p})
        for d, p in others(1)
    ]
    late, last = 3 * share + 1, 4 * share + 1
    cuts_n = ((0, 2 * share, 6, 8), (2 * share, late, 5, 8), (late, last, 7, 8))
    cuts_s = ((0, late, 0, 2), (late, last, 0, 1))

    def rows(cuts, ss, rs, dev, d, p):
        return [
            copy(
                stage.at[p, a:b, lo:hi], tall.at[col, a:b, ROWS + lo : ROWS + hi],
                ss.at[i, d], rs.at[i, d], dict(dev, lon=p),
            )
            for i, (a, b, lo, hi) in enumerate(cuts)
        ]

    rows_n = [rows(cuts_n if d else ((0, last, 5, 8),), n_ss, n_rs, to_n, d, p) for d, p in others(0)]
    rows_s = [rows(cuts_s if d else ((0, last, 0, 2),), s_ss, s_rs, to_s, d, p) for d, p in others(0)]
    depth_n = [copy(n_hbm.at[6:8], cnt.at[14:16], k_ss.at[0], k_rs.at[0], to_n)]
    depth_s = [copy(n_hbm.at[0:2], cnt.at[8:10], k_ss.at[1], k_rs.at[1], to_s)]
    near_n = [copy(c_hbm.at[:, :, 7, :], row_s.at[0], c_ss.at[0], c_rs.at[0], to_n)]
    near_s = [copy(c_hbm.at[:, :, 0, :], row_n.at[0], c_ss.at[1], c_rs.at[1], to_s)]
    far_n = [copy(c_hbm.at[:, :, 6, :], row_s.at[1], c_ss.at[2], c_rs.at[2], to_n)]
    far_s = [copy(c_hbm.at[:, :, 1, :], row_n.at[1], c_ss.at[3], c_rs.at[3], to_s)]
    edge_e = [copy(send_e, got_w, c_ss.at[4], c_rs.at[4], {"lon": lon_e})]
    edge_w = [copy(send_w, got_e, c_ss.at[5], c_rs.at[5], {"lon": lon_w})]
    corners = [
        (copy(col_ed.at[:, 7, :], cor.at[1, 1], q_ss.at[0], q_rs.at[0], dict(to_n, lon=lon_e)), has_n & has_e, has_s & has_w),
        (copy(col_ed.at[:, 7, :], cor.at[1, 0], q_ss.at[1], q_rs.at[1], dict(to_n, lon=lon_w)), has_n & has_w, has_s & has_e),
        (copy(col_ed.at[:, 0, :], cor.at[0, 1], q_ss.at[2], q_rs.at[2], dict(to_s, lon=lon_e)), has_s & has_e, has_n & has_w),
        (copy(col_ed.at[:, 0, :], cor.at[0, 0], q_ss.at[3], q_rs.at[3], dict(to_s, lon=lon_w)), has_s & has_w, has_n & has_e),
    ]
    flow_out = [
        copy(o_send.at[0:2, pl.ds(p * share, share)], out.at[0:2, :, :, cols(col)], uv_ss.at[d], uv_rs.at[d], {"lon": p})
        for d, p in others(1)
    ]
    warm_out = [
        copy(o_send.at[2, pl.ds(p * share, share)], out.at[2, :, :, cols(col)], t_ss.at[d], t_rs.at[d], {"lon": p})
        for d, p in others(1)
    ]
    heat_out = [
        copy(o_send.at[3, pl.ds(p * share, share)], out.at[3, :, :, cols(col)], h_ss.at[d], h_rs.at[d], {"lon": p})
        for d, p in others(1)
    ]

    lane = lax.broadcasted_iota(jnp.int32, (ROWS, LANES), 1)
    row = lax.broadcasted_iota(jnp.int32, (ROWS, LANES), 0)
    eastern, western = lane % STEP == 0, lane % STEP == STEP - 1

    def spots(axis):
        return lax.broadcasted_iota(jnp.int32, (LANES, LANES), axis)

    def twice(mask):
        one = mask.astype(F32).astype(jnp.bfloat16)
        return jnp.concatenate([one, one], axis=0)

    far_lane = (spots(1) + STEP // 2) % STEP
    take = twice(spots(0) == (far_lane + LANES - STEP // 2) % LANES)
    give = twice(
        ((spots(0) % STEP == 0) & (spots(1) == LANES - 1)) | ((spots(0) % STEP == STEP - 1) & (spots(1) == 0))
    )

    def unpack(a, b):
        parts = halves(jnp.concatenate([a, b], axis=0))
        place = lax.broadcasted_iota(jnp.int32, (1, WIDE), 1) % LANES
        only = [
            ((place + 1) % LANES // STEP == t).astype(F32).astype(jnp.bfloat16) for t in range(tracers)
        ]
        e = jnp.dot(jnp.concatenate([parts * o for o in only], axis=0), give, preferred_element_type=F32)
        return [[e[(2 * t + i) * ROWS : (2 * t + i + 1) * ROWS] for i in range(2)] for t in range(tracers)]

    for load in strip_loads:
        load.wait()
    blank = jnp.zeros((ROWS, LANES), F32)
    for p in range(nlon):
        acc = blank
        for f in range(4):
            for l in range(share):
                g = GROUP * (f * share + l)
                e = stage[p + 1, slot(f, l)] if p < nlon - 1 else blank
                w = stage[p - 1, slot(f, l)] if p > 0 else blank
                both = jnp.where(lane < LANES // 2, e, w)
                acc = jnp.where((lane + (3 + LANES - g)) % LANES < 5, pltpu.roll(both, g, 1), acc)
        stage[p, 3 * share] = acc

    pl.semaphore_wait(barrier, nlon - 1 + nlon * (jnp.minimum(s, 1) + jnp.minimum(nstrip - 1 - s, 1)))
    start(has_n, sum(rows_n[1:], []))
    start(has_s, sum(rows_s[1:], []))
    start(None, x_main)
    start(has_n, rows_n[0] + depth_n)
    start(has_s, rows_s[0] + depth_s)

    loads[1].wait()
    for k in range(depth):
        picked = jnp.dot(
            jnp.concatenate([halves(c_in[t, k]) for t in range(tracers)], axis=0), take, preferred_element_type=F32
        )
        acc = picked[0:ROWS]
        for t in range(1, tracers):
            here = (lane >= STEP * t - 2) & (lane < STEP * t + 2)
            acc = jnp.where(here, picked[t * ROWS : (t + 1) * ROWS], acc)
        col_ed[k] = acc
        if k % PAIR == 0:
            even = acc
        else:
            moved = pltpu.roll(acc, STEP // 2, 1)
            send_w[k // PAIR] = jnp.where(lane % STEP < 2, even, moved)
            send_e[k // PAIR] = jnp.where(lane % STEP < 2, moved, even)
    start(has_e, edge_e)
    start(has_w, edge_w)
    start(has_n, near_n)
    start(has_s, near_s)
    for c, send, _ in corners:
        start(send, [c])
    start(has_n, far_n)
    start(has_s, far_s)

    @pl.when(jnp.logical_not(has_s))
    def _():
        tall[:, :, 13:16, :] = jnp.zeros((nlon, 4 * share + 1, 3, LANES), F32)
        cnt[14:16, :] = jnp.zeros((2, nlon * LANES), jnp.int32)
        row_s[...] = jnp.zeros_like(row_s)

    @pl.when(jnp.logical_not(has_n))
    def _():
        tall[:, :, 8:10, :] = jnp.zeros((nlon, 4 * share + 1, 2, LANES), F32)
        cnt[8:10, :] = jnp.zeros((2, nlon * LANES), jnp.int32)
        row_n[...] = jnp.zeros_like(row_n)

    @pl.when(jnp.logical_not(has_w))
    def _():
        got_w[...] = jnp.zeros_like(got_w)

    @pl.when(jnp.logical_not(has_e))
    def _():
        got_e[...] = jnp.zeros_like(got_e)

    for i, there in enumerate((has_n, has_s)):
        for j, beside in enumerate((has_e, has_w)):

            @pl.when(jnp.logical_not(there & beside))
            def _(i=i, j=j):
                cor[i, j] = jnp.zeros((depth, LANES), F32)

    loads[0].wait()
    loads[2].wait()
    tall[col, :, 0:ROWS] = stage[col]
    lead_rates = [jnp.broadcast_to(r_in[0:1, b : b + 1], (ROWS, LANES)) for b in range(tracers)]

    high = tracers * ROWS
    spread = (
        lax.broadcasted_iota(jnp.int32, (high, tracers), 0) // ROWS
        == lax.broadcasted_iota(jnp.int32, (high, tracers), 1)
    ).astype(F32)
    gather = (
        lax.broadcasted_iota(jnp.int32, (tracers, high), 1) // ROWS
        == lax.broadcasted_iota(jnp.int32, (tracers, high), 0)
    ).astype(F32)
    rates = jnp.dot(
        spread, jnp.dot(r_in[...], gather, precision=EXACT, preferred_element_type=F32),
        precision=EXACT, preferred_element_type=F32,
    )
    same_row = (
        lax.broadcasted_iota(jnp.int32, (high, high), 0) % ROWS
        == lax.broadcasted_iota(jnp.int32, (high, high), 1) % ROWS
    )
    rates = split(jnp.where(same_row, rates, 0.0))
    spot0 = lax.broadcasted_iota(jnp.int32, (LANES, tracers), 0)
    pick0 = ((spot0 + 1) % LANES // STEP == lax.broadcasted_iota(jnp.int32, (LANES, tracers), 1)).astype(F32)
    spot1 = lax.broadcasted_iota(jnp.int32, (tracers, LANES), 1)
    pick1 = ((spot1 + 1) % LANES // STEP == lax.broadcasted_iota(jnp.int32, (tracers, LANES), 0)).astype(F32)
    across = jnp.dot(
        lax.dot_general(
            pick0, r_in[...], (((1,), (1,)), ((), ())), precision=EXACT, preferred_element_type=F32
        ),
        pick1, precision=EXACT, preferred_element_type=F32,
    )
    side_a = lax.broadcasted_iota(jnp.int32, (LANES, LANES), 0) % STEP
    side_b = lax.broadcasted_iota(jnp.int32, (LANES, LANES), 1) % STEP
    across = split(jnp.where((side_a == side_b) & ((side_a == 0) | (side_a == STEP - 1)), across, 0.0))

    for k in range(depth):
        for t in range(tracers):
            c_east[t, k] = pltpu.roll(c_in[t, k], LANES - 1, 1)
            c_west[t, k] = pltpu.roll(c_in[t, k], 1, 1)

    wait_recv(has_s, rows_n[0] + depth_n)
    wait_recv(has_n, rows_s[0] + depth_s)

    lane2 = lax.broadcasted_iota(jnp.int32, (EXT, LANES), 1)
    window = (lane2 < 2) | (lane2 >= LANES - 3)

    def field(f, q, l):
        g = GROUP * (f * share + l)
        held = tall[q, 3 * share]
        moved = pltpu.roll(held, (LANES - g) % LANES, 1) if g else held
        return jnp.concatenate([tall[q, slot(f, l)], jnp.where(window, moved, 0.0)], axis=1)

    wet_e = jnp.where((lane2 < 2) & has_e, cnt[:, cols(lon_e)], 0)
    wet_w = jnp.where((lane2 >= LANES - 3) & has_w, cnt[:, cols(lon_w)], 0)
    n_main = cnt[:, cols(col)]
    n_side = jnp.where(lane2 < LANES // 2, wet_e, wet_w)
    layers = jnp.concatenate([n_main, n_side], axis=1)
    level_main = n_main[0:ROWS]

    line = lax.broadcasted_iota(jnp.int32, (EXT, WIDE), 0)
    spot = (s * ROWS + jnp.where(line < 12, line, line - EXT)).astype(F32)
    fcor = 0.3 * (2.0 * (spot + 0.5) / (nstrip * ROWS) - 1.0)

    layers_u, layers_v = jnp.minimum(layers, east(layers)), jnp.minimum(layers, north(layers))

    def masks(k):
        return [(k < n).astype(F32) for n in (layers, layers_u, layers_v)]

    def advance(m, u, v, t):
        push = 0.2 * t
        new_u = m[1] * (0.6 * u + east(0.1 * u - push) + 0.1 * (west(u) + north(u) + south(u)) + fcor * v + push)
        new_v = m[2] * (0.6 * v + north(0.1 * v - push) + 0.1 * (east(v) + west(v) + south(v)) - fcor * u + push)
        return new_u, new_v

    def both(x):
        return jnp.where(eastern, jnp.broadcast_to(x[:, 0:1], x.shape), jnp.broadcast_to(x[:, LANES - 1 :], x.shape))

    def both_steps(q):
        for l in range(share):
            k = q * share + l
            m = masks(k)
            u0, v0, t0, h0 = (field(f, q, l) for f in range(4))
            u1, v1 = advance(m, u0, v0, t0)
            for i, a in enumerate(upwind(u1, west(u1), v1, south(v1))):
                cex[i, k] = a[:, 0:LANES]
                cec[i, k] = both(a[0:ROWS, LANES:WIDE])
            t1 = m[0] * (t0 + 0.1 * lap(t0) + 0.5 * h0)
            u2, v2 = advance(m, u1, v1, t1)
            u_here, v_here = u2[0:ROWS, 0:LANES], v2[0:ROWS, 0:LANES]
            u_back, v_back = west(u2)[0:ROWS, 0:LANES], south(v2)[0:ROWS, 0:LANES]
            for i, a in enumerate(upwind(u_here, u_back, v_here, v_back)):
                cf1[i, k] = a
            t_base[k] = (m[0] * (t1 + 0.1 * lap(t1)))[0:ROWS, 0:LANES]
            o_send[0, k] = u_here
            o_send[1, k] = v_here

    both_steps(col)
    for d, _ in others(1):
        wait_recv(has_s, rows_n[d])
        wait_recv(has_n, rows_s[d])
        wait_recv(None, x_main[d - 1 : d])
        both_steps(lax.rem(col + nlon - d, nlon))
    start(None, flow_out)
    out[0:2, :, :, cols(col)] = o_send[0:2, mine]

    def coefs(m, k):
        if m == 0:
            return [cex[i, k, 0:ROWS, :] for i in range(5)]
        return [cf1[i, k] for i in range(5)]

    def advect(a, x, edge, above, below, x_e=None, x_w=None):
        if x_e is None:
            x_e, x_w = pltpu.roll(x, LANES - 1, 1), pltpu.roll(x, 1, 1)
        x_n = jnp.where(row == ROWS - 1, above, pltpu.roll(x, ROWS - 1, 0))
        x_s = jnp.where(row == 0, below, pltpu.roll(x, 1, 0))
        x_e = jnp.where(lane == LANES - 1, edge, x_e)
        x_w = jnp.where(lane == 0, edge, x_w)
        return mix(a, x, x_e, x_w, x_n, x_s)

    def lead_of(values):
        parts = [v * a for v, a in zip(values, lead_rates)]
        while len(parts) > 1:
            parts = [sum(parts[i : i + 2]) for i in range(0, len(parts), 2)]
        return parts[0]

    def shine(m, leads):
        tau, top = jnp.zeros((ROWS, LANES), F32), jnp.ones((ROWS, LANES), F32)
        tops = []
        for k, lead in enumerate(leads):
            wet_k = (k < level_main).astype(F32)
            tau = tau + (0.1 + 0.3 * jnp.maximum(lead, 0.0))
            under = jnp.exp(-tau)
            heat = 2.0 * wet_k * (top - under)
            if m == 0:
                o_send[2, k] = t_base[k] + 0.5 * wet_k * heat
            else:
                o_send[3, k] = heat
            tops.append(top)
            top = under
        start(None, heat_out if m else warm_out)
        out[2 + m, :, :, cols(col)] = o_send[2 + m, mine]
        return tops

    def react(blocks):
        parts = [split(a) for a in blocks]
        r = product(
            rates, (jnp.concatenate([a for a, _ in parts], axis=1), jnp.concatenate([b for _, b in parts], axis=1))
        )
        return [r[:, i * LANES : (i + 1) * LANES].reshape(tracers, ROWS, LANES) for i in range(len(blocks))]

    def settle(k, top, value, gain):
        return (k < level_main).astype(F32) * (value + (0.5 * top) * gain)

    def sideways(k):
        e, w = got_e[k // PAIR], got_w[k // PAIR]
        if k % PAIR:
            e, w = (pltpu.roll(x, LANES - STEP // 2, 1) for x in (e, w))
        return jnp.where(lane % STEP < 2, e, w)

    def ring_rows():
        tops, wets = [], []
        ends = unpack(*(jnp.where(lane % STEP < 2, cor[i, 0], cor[i, 1]) for i in range(2)))
        for i in range(2):
            rows, line_at, inner = (row_n, 8, 7) if i == 0 else (row_s, 15, 0)
            a = [cex[j, :, line_at, :] for j in range(5)]
            values = []
            for t in range(tracers):
                x, far, near = rows[0, t], rows[1, t], c_in[t, :, inner, :]
                edge = ends[t][i]
                x_e = jnp.where(lane == LANES - 1, edge, pltpu.roll(x, LANES - 1, 1))
                x_w = jnp.where(lane == 0, edge, pltpu.roll(x, 1, 1))
                x_n, x_s = (far, near) if i == 0 else (near, far)
                values.append(mix(a, x, x_e, x_w, x_n, x_s))
                (raw_n, raw_s)[i][t] = values[t]
            tau = 0.1 + 0.3 * jnp.maximum(values[0], 0.0)
            tau = jnp.where(row > 0, pltpu.roll(tau, 1, 0), 0.0)
            for shift in (1, 2, 4):
                tau = tau + jnp.where(row >= shift, pltpu.roll(tau, shift, 0), 0.0)
            top = jnp.exp(-tau)
            wet = (row < n_main[line_at : line_at + 1, :]).astype(F32)
            (lead_n, lead_s)[i][...] = wet * (values[0] + (0.5 * top) * lead_of(values))
            tops.append(top)
            wets.append(wet)
        return tops, wets

    def ring_finish(tops, wets):
        blocks = [a[...] for a in (raw_n, raw_s)]
        gains = react([a.reshape(high, LANES) for a in blocks])
        for i, ring in enumerate((ring_n, ring_s)):
            ring[...] = wets[i] * (blocks[i] + (0.5 * tops[i]) * gains[i])

    def ring_cols():
        edge_n = jnp.where(lane % STEP < 2, cor[0, 0], cor[0, 1])
        edge_s = jnp.where(lane % STEP < 2, cor[1, 0], cor[1, 1])
        wet_n = both(n_side[0:ROWS])
        tau = jnp.zeros((ROWS, LANES), F32)
        values, tops = [], []
        for k in range(depth):
            x, own = sideways(k), col_ed[k]
            a = [cec[i, k] for i in range(5)]
            x_e = pltpu.roll(jnp.where(eastern, own, x), LANES - 1, 1)
            x_w = pltpu.roll(jnp.where(western, own, x), 1, 1)
            x_n = jnp.where(row == ROWS - 1, edge_n[k : k + 1, :], pltpu.roll(x, ROWS - 1, 0))
            x_s = jnp.where(row == 0, edge_s[k : k + 1, :], pltpu.roll(x, 1, 0))
            value = mix(a, x, x_e, x_w, x_n, x_s)
            values.append(value)
            tops.append(jnp.exp(-tau))
            tau = tau + (0.1 + 0.3 * jnp.maximum(both(value), 0.0))
        r = product(split(jnp.concatenate(values, axis=0)), across)
        for k in range(depth):
            wet = (k < wet_n).astype(F32)
            ring_c[k] = wet * (values[k] + (0.5 * tops[k]) * r[k * ROWS : (k + 1) * ROWS])

    groups = [range(g, g + PAIR) for g in range(0, depth, PAIR)]
    wait_recv(has_s, near_n)
    wait_recv(has_n, near_s)
    wait_recv(has_w, edge_e)
    wait_recv(has_e, edge_w)
    leads, firsts = [], []
    for levels in groups:
        edges = unpack(*(sideways(k) for k in levels))
        for i, k in enumerate(levels):
            a = coefs(0, k)
            values = [
                advect(
                    a, c_in[t, k], edges[t][i], row_n[0, t, k : k + 1, :], row_s[0, t, k : k + 1, :],
                    c_east[t, k], c_west[t, k],
                )
                for t in range(tracers)
            ]
            for t in range(tracers):
                c_raw[t, k] = values[t]
            leads.append(values[0])
            firsts.append(lead_of(values))
    tops = shine(0, leads)
    for k in range(depth):
        lead_c[k] = settle(k, tops[k], leads[k], firsts[k])

    wait_recv(has_s, far_n)
    wait_recv(has_n, far_s)
    for c, _, recv in corners:
        wait_recv(recv, [c])
    ring_cols()
    ring_light = ring_rows()
    leads = []
    for k in range(depth):
        x, beside = lead_c[k], ring_c[k]
        x_n = jnp.where(row == ROWS - 1, lead_n[k : k + 1, :], pltpu.roll(x, ROWS - 1, 0))
        x_s = jnp.where(row == 0, lead_s[k : k + 1, :], pltpu.roll(x, 1, 0))
        x_e = pltpu.roll(jnp.where(lane == 0, beside, x), LANES - 1, 1)
        x_w = pltpu.roll(jnp.where(lane == LANES - 1, beside, x), 1, 1)
        leads.append(mix(coefs(1, k), x, x_e, x_w, x_n, x_s))
    last = shine(1, leads)

    ring_finish(*ring_light)
    for levels in groups:
        blocks = [c_raw[:, k] for k in levels]
        gains = react([b.reshape(high, LANES) for b in blocks])
        for k, block, gain in zip(levels, blocks, gains):
            c_mid[:, k] = settle(k, tops[k], block, gain)
    for levels in groups:
        edges = unpack(*(ring_c[k] for k in levels))
        blocks = []
        for i, k in enumerate(levels):
            a = coefs(1, k)
            blocks.append(jnp.concatenate([leads[k]] + [
                advect(a, c_mid[t, k], edges[t][i], ring_n[t, k : k + 1, :], ring_s[t, k : k + 1, :])
                for t in range(1, tracers)
            ], axis=0))
        gains = react(blocks)
        for k, block, gain in zip(levels, blocks, gains):
            c_out[:, k] = settle(k, last[k], block.reshape(tracers, ROWS, LANES), gain)

    wait_send(None, x_main)
    wait_send(has_n, sum(rows_n, []) + depth_n + near_n + far_n)
    wait_send(has_s, sum(rows_s, []) + depth_s + near_s + far_s)
    wait_send(has_e, edge_e)
    wait_send(has_w, edge_w)
    for c, send, _ in corners:
        wait_send(send, [c])
    wait_send(None, flow_out + warm_out)
    wait_recv(None, flow_out + warm_out)
    wait_send(None, heat_out)
    wait_recv(None, heat_out)


def store(out, c_out, u_dst, v_dst, t_dst, h_dst, c_dst, sem):
    saves = [pltpu.make_async_copy(c_out, c_dst, sem.at[4])]
    saves += [pltpu.make_async_copy(out.at[i], b, sem.at[i]) for i, b in enumerate((u_dst, v_dst, t_dst, h_dst))]
    for save in saves:
        save.start()
    for save in saves:
        save.wait()


def shards(sizes, u, v, t, h, c, n, r):
    tracers, depth, share, nlon, _, _ = sizes
    width = nlon * LANES
    strip = jax.ShapeDtypeStruct(u.shape, F32)
    tile = (ROWS, LANES)
    dma = pltpu.SemaphoreType.DMA
    hbm = pl.BlockSpec(memory_space=pltpu.HBM)
    vmem = pl.BlockSpec(memory_space=pltpu.VMEM)
    buf = pltpu.VMEM
    line = (tracers, depth, LANES)
    pair = [dma((nlon,)), dma((nlon,))]
    held = pl.pallas_call(
        functools.partial(kernel, sizes),
        out_shape=(buf((4, share, ROWS, width), F32), buf(c.shape, F32)),
        in_specs=[hbm] * 7,
        out_specs=(vmem, vmem),
        scratch_shapes=[
            buf((nlon, 4 * share + 1) + tile, F32),
            buf((nlon, 4 * share + 1, EXT, LANES), F32),
            buf((2, depth, EXT, WIDE), F32),
            buf((EXT, width), jnp.int32),
            *([buf(c.shape, F32)] * 5),
            buf((2,) + line, F32), buf((2,) + line, F32),
            buf(line, F32), buf(line, F32), buf(line, F32), buf(line, F32),
            buf((depth,) + tile, F32), *([buf((depth // PAIR,) + tile, F32)] * 4),
            buf((2, 2, depth, LANES), F32),
            buf((depth,) + tile, F32), buf((depth,) + tile, F32), buf((depth, LANES), F32), buf((depth, LANES), F32),
            buf((5, depth, EXT, LANES), F32),
            buf((5, depth) + tile, F32),
            buf((5, depth) + tile, F32),
            buf((depth,) + tile, F32),
            buf((4, depth) + tile, F32),
            buf(r.shape, F32),
            dma((3,)), dma((4, nlon)),
            *pair, dma((3, nlon)), dma((3, nlon)), dma((2, nlon)), dma((2, nlon)),
            dma((2,)), dma((2,)), dma((6,)), dma((6,)), dma((4,)), dma((4,)),
            *(pair * 3),
        ],
        compiler_params=pltpu.CompilerParams(
            collective_id=0, has_side_effects=True, vmem_limit_bytes=VMEM
        ),
    )(*(pltpu.with_memory_space_constraint(x, pltpu.HBM) for x in (u, v, t, h, c, n, r)))
    return pl.pallas_call(
        store,
        out_shape=(strip, strip, strip, strip, jax.ShapeDtypeStruct(c.shape, F32)),
        in_specs=[vmem] * 2,
        out_specs=(hbm,) * 5,
        scratch_shapes=[dma((5,))],
        compiler_params=pltpu.CompilerParams(vmem_limit_bytes=VMEM),
    )(*held)


def solution(mesh):
    nlon, nrole = mesh.shape["lon"], mesh.shape["role"]
    nstrip = mesh.shape["lat"] * nrole
    strip = P("lon", ("grp", "lat", "role"), None)
    tile = P(None, None, ("grp", "lat", "role"), "lon")

    def run(u, v, t, h, c, n, r):
        sizes = (c.shape[0], c.shape[1], u.shape[0] // nlon, nlon, nrole, nstrip)
        return jax.shard_map(
            functools.partial(shards, sizes),
            mesh=mesh,
            in_specs=(strip, strip, strip, strip, tile, P(("grp", "lat", "role"), None), P()),
            out_specs=(strip, strip, strip, strip, tile),
            check_vma=False,
        )(u, v, t, h, c, n, r)

    return run
```
